32 devices in a mesh: voxel: 2 (over x), feature: 4 (over z), tm: 4 (over y, core).
Axes of the slice: x: 2, y: 2, z: 4, core: 2. Of those that a mesh axis runs over, the one named last changes fastest.
Arguments:
- hidden: bfloat16 [3072, 8192], P('tm', 'feature'), may hold values from -6 to 6
- bold: bfloat16 [3072, 256], P('tm', 'voxel'), may hold values from -6 to 6
- panel: bfloat16 [65536, 128], P(('feature', 'tm'), 'voxel'), may hold values from -0.0234375 to 0.0234375
- eigvals: float32 [128], replicated, may hold values from 0.05 to 2
- ridge_grid: int32 [24], replicated, may hold values from 0 to 16
- delays: int32 [8], replicated, may hold values from 1 to 12, as said below
- runs: int32 [3072], replicated, may hold values from 0 to 7, never falling along the last dimension, each value on 1 to 768 neighbouring positions
Outputs:
- scaled: bfloat16 [24, 128, 256], P(None, None, 'voxel')
The draws below stay inside these ranges and needn't reach their ends.
Inputs may be any that keep to these rules, and one draw needn't show every extreme that they name: 8 distinct delays, 12 among them. `runs`: run numbers never fall along the TRs; a run holds 1 to 768 TRs.
All inputs are finite; a program needn't handle non-finite values.
Results may differ from the reference program's by a relative error of at most 0.022.
Values may be sent and summed in bfloat16 or wider, within the bound.
No kernel may reach another device: no remote copies, remote signals or barrier semaphores. Data moves between devices by JAX's collectives and lax.ppermute only.
A program may use at most 64 MiB of HBM per device.

```python
import math
import jax
import jax.numpy as jnp
import numpy as np
from jax import lax

D = 8192
DELAYS = 8
MAXD = 12
T_DEV = 768
V_DEV = 128
PANEL = 128
RIDGES = 24
FEATS = 65536
TRS = 3072
VOX = 256
N_TM = 4


def draw_delays(key, part):
    others = jax.random.permutation(key, MAXD - 1) + 1
    picked = jnp.concatenate([jnp.full((1,), MAXD, jnp.int32), others[:DELAYS - 1].astype(jnp.int32)])
    return jax.random.permutation(jax.random.fold_in(key, 7), picked).astype(jnp.int32)


def place_ends(entries, key, low, top_value):
    place = [jax.random.randint(jax.random.fold_in(key, axis), (), 0, length) for axis, length in enumerate(entries.shape)]
    main_axis = entries.shape.index(max(entries.shape))
    neighbour = place[:main_axis] + [(place[main_axis] + 1) % entries.shape[main_axis]] + place[main_axis + 1:]
    return entries.at[tuple(place)].set(low).at[tuple(neighbour)].set(top_value)


def block_scale(rng, dims, split, least, high):
    loudness = 1.0
    for dim, shards_of in split:
        draws = jax.random.uniform(jax.random.fold_in(jax.random.fold_in(rng, 6), dim), (shards_of,), jnp.float32, least / len(split), high / len(split))
        loudness = loudness * jnp.repeat(jnp.exp(draws), dims[dim] // shards_of).reshape((-1,) + (1,) * (len(dims) - 1 - dim))
    return loudness


def split_up(number_of, total, bound, slope):
    weights = [(1 << 20) // math.isqrt(rank ** slope) + 1 for rank in range(2, number_of + 1)]
    surplus, holding = total - bound - (number_of - 1), [1] * (number_of - 1)
    while surplus > 0:
        candidates = [i for i in range(number_of - 1) if holding[i] < bound]
        whole, remaining = sum([weights[i] for i in candidates]), surplus
        for i in candidates:
            extra = min(bound - holding[i], max(1, remaining * weights[i] // whole), surplus)
            holding[i] = holding[i] + extra
            surplus = surplus - extra
    return np.array([bound] + holding)


def ragged(key, amount, total, limit, skew):
    if amount == 2:
        one = jax.random.randint(key, (), max(1, total - limit), min(limit, total - 1) + 1)
        return jnp.stack([one, total - one])
    lengths = jnp.asarray(split_up(amount, total, limit, skew), jnp.int32)
    twos = (amount - 1) // 2
    source_of, receiver = lengths[1:1 + 2 * twos:2], lengths[2:2 + 2 * twos:2]
    slack = jnp.minimum(source_of - 1, limit - receiver)
    shifted = jax.random.randint(jax.random.fold_in(key, 1), (twos,), 0, 1 << 20) % (slack + 1)
    lengths = lengths.at[1:1 + 2 * twos:2].set(source_of - shifted).at[2:2 + 2 * twos:2].set(receiver + shifted)
    return lengths[jax.random.permutation(jax.random.fold_in(key, 2), amount)]


def normal_values(rng, extent, deviation, limit, shards=(), held_as=jnp.bfloat16):
    loudness = block_scale(rng, extent, shards, -0.22, 0.18) if shards else 1.0
    entries = jax.random.normal(rng, extent, jnp.float32) * deviation * loudness
    return jnp.minimum(jnp.maximum(entries, -limit), limit).astype(held_as)


def setup_inputs(seed: int = 0) -> dict:
    keys = jax.random.split(jax.random.key(seed), 8)
    return {
        "hidden": normal_values(keys[0], (TRS, D), 1.0, 6.0, ((0, 4), (1, 4))),
        "bold": normal_values(keys[1], (TRS, VOX), 1.0, 6.0, ((0, 4), (1, 2))),
        "panel": normal_values(keys[2], (FEATS, PANEL), FEATS ** -0.5, 0.0234375, ((0, 16), (1, 2))),
        "eigvals": jnp.clip(jnp.exp(jax.random.uniform(keys[3], (PANEL,), jnp.float32, math.log(0.05), math.log(2.0))), 0.05, 2.0),
        "ridge_grid": place_ends(jax.random.randint(keys[4], (RIDGES,), 0, 17), jax.random.fold_in(keys[4], 1), 0, 16).astype(jnp.int32),
        "delays": draw_delays(jax.random.fold_in(keys[7], 71), 0),
        "runs": jnp.searchsorted(jnp.cumsum(ragged(keys[6], 2 * N_TM, TRS, T_DEV, 2)), jnp.arange(TRS), side="right").astype(jnp.int32),
    }


def reference(hidden, bold, panel, eigvals, ridge_grid, delays, runs):
    steps_idx = jnp.arange(TRS, dtype=jnp.int32)
    runs_pad = jnp.concatenate([runs, jnp.full((MAXD,), -1, jnp.int32)])
    bold_pad = jnp.concatenate([bold, jnp.zeros((MAXD, VOX), jnp.bfloat16)], 0)
    lagged_list = []
    for slot in range(DELAYS):
        target = steps_idx + delays[slot]
        valid = (target < TRS) & (runs_pad[target] == runs)
        moved = bold_pad[target]
        lagged_list.append(jnp.where(valid[:, None], moved, jnp.zeros_like(moved)))
    lagged = jnp.stack(lagged_list, 1)
    basis = panel.astype(jnp.float32)
    blocks = VOX // V_DEV

    def one_block(index):
        start = (index * V_DEV).astype(jnp.int32)
        piece = lax.dynamic_slice_in_dim(lagged, start, V_DEV, 2)
        total = jnp.zeros((PANEL, V_DEV), jnp.float32)
        for shard in range(N_TM):
            rows_x = hidden[shard * T_DEV:(shard + 1) * T_DEV].astype(jnp.float32)
            rows_y = piece[shard * T_DEV:(shard + 1) * T_DEV].reshape(T_DEV, DELAYS * V_DEV).astype(jnp.float32)
            cross = jnp.dot(rows_x.T, rows_y, precision=lax.Precision.HIGHEST)
            partial_value = cross.reshape(D * DELAYS, V_DEV).astype(jnp.bfloat16).astype(jnp.float32)
            total = total + jnp.dot(basis.T, partial_value, precision=lax.Precision.HIGHEST)
        return total
    stacked = lax.map(one_block, jnp.arange(blocks, dtype=jnp.int32))
    rotated = jnp.transpose(stacked, (1, 0, 2)).reshape(PANEL, VOX)
    penalty = 2.0 ** ((ridge_grid.astype(jnp.float32) - 8.0) * 0.5)
    scaled = rotated[None] / (math.sqrt(TRS) * (eigvals[None, :, None] + penalty[:, None, None]))
    return scaled.astype(jnp.bfloat16)
```

```python
import functools
import math

import jax
import jax.numpy as jnp
from jax import lax
from jax.experimental import pallas as pl
from jax.experimental.pallas import tpu as pltpu
from jax.sharding import PartitionSpec as P

DELAYS = 8
MAXD = 12
LANES = 128
F32 = jnp.float32
BF16 = jnp.bfloat16


def passed_along(value, axis, steps):
    count = lax.axis_size(axis)
    first, last = (max(0, -steps), min(count, count - steps))
    return lax.ppermute(value, axis, [(source, source + steps) for source in range(first, last)])


def contract_rows(left, right):
    return lax.dot_general(
        left, right, (((0,), (0,)), ((), ())), preferred_element_type=jnp.float32
    )


def scaled_by(rotated, eigvals, ridge_grid, total_rows):
    penalty = 2.0 ** ((ridge_grid.astype(jnp.float32) - 8.0) * 0.5)
    scaled = rotated[None] / (
        math.sqrt(total_rows) * (eigvals[None, :, None] + penalty[:, None, None])
    )
    return scaled.astype(jnp.bfloat16)


def gathered(hidden, bold, panel, eigvals, ridge_grid, delays, runs):
    t_rows = hidden.shape[0]
    d_local = hidden.shape[1]
    v_cols = bold.shape[1]
    total_rows = t_rows * lax.axis_size("tm")
    first = lax.axis_index("tm") * t_rows
    ahead = passed_along(bold[:MAXD], "tm", -1)
    extended = jnp.concatenate([bold, ahead], 0)
    runs_pad = jnp.concatenate([runs, jnp.full((MAXD,), -1, jnp.int32)])
    own_runs = lax.dynamic_slice_in_dim(runs, first, t_rows)
    positions = first + jnp.arange(t_rows, dtype=jnp.int32)
    lagged_list = []
    for slot in range(DELAYS):
        offset = delays[slot]
        target_runs = lax.dynamic_slice_in_dim(runs_pad, first + offset, t_rows)
        valid = (positions + offset < total_rows) & (target_runs == own_runs)
        moved = lax.dynamic_slice_in_dim(extended, offset, t_rows, 0)
        lagged_list.append(jnp.where(valid[:, None], moved, jnp.zeros_like(moved)))
    stacked = jnp.stack(lagged_list, 1).reshape(t_rows, DELAYS * v_cols)
    cross = contract_rows(hidden, stacked)
    partial_cov = cross.reshape(d_local * DELAYS, v_cols).astype(jnp.bfloat16)
    panel_rows = lax.all_gather(panel, "tm", axis=0, tiled=True)
    rotated_part = contract_rows(
        lax.all_gather(panel_rows, "voxel", axis=1, tiled=True), partial_cov
    )
    rotated = lax.psum(rotated_part.astype(jnp.bfloat16), ("feature", "tm")).astype(jnp.float32)
    return scaled_by(rotated, eigvals, ridge_grid, total_rows)


def swapped(value, voxel, feature, tm):
    sizes = (lax.axis_size("voxel"), lax.axis_size("feature"), lax.axis_size("tm"))
    pairs = []
    for v in range(sizes[0]):
        for f in range(sizes[1]):
            for t in range(sizes[2]):
                source = (v * sizes[1] + f) * sizes[2] + t
                target = ((v ^ voxel) * sizes[1] + (f ^ feature)) * sizes[2] + (t ^ tm)
                pairs.append((source, target))
    return lax.ppermute(value, ("voxel", "feature", "tm"), pairs)


def lag_sums(scalars, panel_t, own, other, runs, sort, total, ordered, products):
    p_cols = panel_t.shape[0]
    rows, width = own.shape
    block = DELAYS * LANES
    groups = width // LANES
    core = scalars[DELAYS]
    stacked = jnp.concatenate([panel_t[:, g * block:(g + 1) * block] for g in range(groups)], 0)
    by_slot = jnp.dot(stacked, sort[...], preferred_element_type=F32).astype(BF16)
    for g in range(groups):
        for k in range(DELAYS):
            ordered[k * p_cols:(k + 1) * p_cols, g * LANES:(g + 1) * LANES] = by_slot[
                g * p_cols:(g + 1) * p_cols, k * LANES:(k + 1) * LANES
            ]
    span = 2 * rows
    products[:, :LANES] = jnp.zeros((DELAYS * p_cols, LANES), F32)
    products[:, LANES + span:] = jnp.zeros((DELAYS * p_cols, LANES), F32)
    for part, place in ((own, core), (other, 1 - core)):
        products[:, pl.ds(pl.multiple_of(LANES + place * rows, LANES), rows)] = lax.dot_general(
            ordered[...], part[...], (((1,), (1,)), ((), ())), preferred_element_type=F32
        )
    tiles = span // LANES + 1
    lane = lax.broadcasted_iota(jnp.int32, (8, LANES), 1)
    here = runs[...]
    kept = []
    for k in range(DELAYS):
        kept.append((pltpu.roll(here, scalars[k], 1) == here).astype(F32))
    for row in range(0, p_cols, 8):
        sums = [total[row:row + 8, j * LANES:(j + 1) * LANES] for j in range(tiles)]
        for k in range(DELAYS):
            low = lane < scalars[k]
            before = None
            for j in range(tiles):
                at = k * p_cols + row
                now = pltpu.roll(
                    products[at:at + 8, (j + 1) * LANES:(j + 2) * LANES], scalars[k], 1
                )
                if before is None:
                    moved = jnp.where(low, 0.0, now)
                else:
                    moved = jnp.where(low, before, now)
                before = now
                sums[j] = sums[j] + moved * kept[k][:, j * LANES:(j + 1) * LANES]
        for j in range(tiles):
            total[row:row + 8, j * LANES:(j + 1) * LANES] = sums[j]


def first_kernel(scalars, panel_t, own, other, runs, sort, total, ordered, products):
    total[...] = jnp.zeros_like(total)
    lag_sums(scalars, panel_t, own, other, runs, sort, total, ordered, products)


def last_kernel(
    scalars, panel_t, own, other, runs, sort, earlier, bold_own, bold_core, bold_x, bold_xcore, ahead,
    out, total, ordered, products,
):
    total[...] = earlier[...]
    lag_sums(scalars, panel_t, own, other, runs, sort, total, ordered, products)
    rows = own.shape[0]
    core = scalars[DELAYS]
    v_cols = bold_own.shape[1]
    mine = total[:, pl.ds(pl.multiple_of(core * rows, LANES), rows)].astype(BF16)
    theirs = total[:, pl.ds(pl.multiple_of((1 - core) * rows, LANES), rows)].astype(BF16)
    beyond = total[:, 2 * rows:2 * rows + LANES].astype(BF16)
    for place, (a, b) in enumerate(((bold_own, bold_core), (bold_x, bold_xcore))):
        out[:, place * v_cols:(place + 1) * v_cols] = (
            jnp.dot(mine, a[...], preferred_element_type=F32)
            + jnp.dot(theirs, b[...], preferred_element_type=F32)
            + jnp.dot(
                beyond, ahead[:, place * v_cols:(place + 1) * v_cols], preferred_element_type=F32
            )
        )


def call(kernel, operands, out_shape, scratch, flops):
    vmem = pl.BlockSpec(memory_space=pltpu.VMEM)
    smem = pl.BlockSpec(memory_space=pltpu.SMEM)
    return pl.pallas_call(
        kernel,
        out_shape=out_shape,
        in_specs=[smem] + [vmem] * (len(operands) - 1),
        out_specs=vmem,
        scratch_shapes=scratch,
        compiler_params=pltpu.CompilerParams(vmem_limit_bytes=40 * 1024 * 1024),
        cost_estimate=pl.CostEstimate(flops=flops, bytes_accessed=8 * 1024 * 1024, transcendentals=0),
    )(*operands)


def exchanged(hidden, bold, panel, eigvals, ridge_grid, delays, runs):
    t_rows, d_local = hidden.shape
    v_cols = bold.shape[1]
    p_cols = panel.shape[1]
    tm_count = lax.axis_size("tm")
    total_rows = t_rows * tm_count
    width = d_local // tm_count
    tm = lax.axis_index("tm")
    chip, core = tm // 2, tm % 2
    voxel = lax.axis_index("voxel")

    panel_t = panel.T
    late_t = swapped(panel_t, 0, 0, 2)

    def columns(block):
        return lax.dynamic_slice_in_dim(hidden, block * width, width, 1)

    early_other = swapped(columns(tm ^ 1), 0, 0, 1)
    late_other = swapped(columns(tm ^ 3), 0, 0, 1)
    bold_x = swapped(bold, 1, 0, 0)
    bold_core = swapped(bold, 0, 0, 1)
    bold_xcore = swapped(bold_x, 0, 0, 1)
    head = jnp.concatenate([
        jnp.where(core == 0, bold[:16], bold_core[:16]),
        jnp.where(core == 0, bold_x[:16], bold_xcore[:16]),
    ], 1)
    head = lax.ppermute(head, "tm", [(t, t - 2) for t in range(2, tm_count)])
    ahead = jnp.concatenate([head, jnp.zeros((LANES - 16, 2 * v_cols), BF16)], 0)

    span = 2 * t_rows
    runs_pad = jnp.concatenate([runs, jnp.full((LANES,), -1, jnp.int32)])
    chip_runs = lax.dynamic_slice_in_dim(runs_pad, chip * span, span + LANES)
    chip_runs = jnp.broadcast_to(chip_runs[None], (8, span + LANES))
    scalars = jnp.concatenate([delays, jnp.full((8,), core, jnp.int32)])
    block = DELAYS * LANES
    row = lax.broadcasted_iota(jnp.int32, (block, block), 0)
    col = lax.broadcasted_iota(jnp.int32, (block, block), 1)
    sort = ((row % DELAYS) * LANES + row // DELAYS == col).astype(BF16)

    scratch = [
        pltpu.VMEM((DELAYS * p_cols, width), BF16),
        pltpu.VMEM((DELAYS * p_cols, span + 2 * LANES), F32),
    ]
    flops = 2 * DELAYS * p_cols * width * span
    total = jax.ShapeDtypeStruct((p_cols, span + LANES), F32)
    early = call(
        first_kernel,
        (scalars, panel_t, columns(tm), early_other, chip_runs, sort),
        total, scratch, flops,
    )
    part = call(
        last_kernel,
        (scalars, late_t, columns(tm ^ 2), late_other, chip_runs, sort, early,
         bold, bold_core, bold_x, bold_xcore, ahead),
        jax.ShapeDtypeStruct((p_cols, 2 * v_cols), F32),
        [pltpu.VMEM((p_cols, span + LANES), F32)] + scratch, flops,
    )

    part = part + swapped(part.astype(BF16), 0, 0, 1).astype(F32)
    mine, theirs = part[:, :v_cols], part[:, v_cols:]
    mine_b, theirs_b = mine.astype(BF16), theirs.astype(BF16)
    from_y = swapped(mine_b, 0, 0, 2)
    from_x = swapped(theirs_b, 1, 0, 0)
    from_xy = swapped(theirs_b, 1, 0, 2)
    near = mine + from_y.astype(F32)
    far = from_x.astype(F32) + from_xy.astype(F32)
    rotated = jnp.where(
        voxel == 0, jnp.concatenate([near, far], 0), jnp.concatenate([far, near], 0)
    )
    rotated = rotated + swapped(rotated.astype(BF16), 0, 1, 0).astype(F32)
    rotated = rotated + swapped(rotated.astype(BF16), 0, 2, 0).astype(F32)
    return scaled_by(rotated, eigvals, ridge_grid, total_rows)


def solution(mesh):
    sizes = (mesh.shape["voxel"], mesh.shape["feature"], mesh.shape["tm"])
    shards = exchanged if sizes == (2, 4, 4) else gathered
    return jax.shard_map(
        shards,
        mesh=mesh,
        in_specs=(
            P("tm", "feature"),
            P("tm", "voxel"),
            P(("feature", "tm"), "voxel"),
            P(),
            P(),
            P(),
            P(),
        ),
        out_specs=P(None, None, "voxel"),
        check_vma=False,
    )
```

```python
import math

import jax
import jax.numpy as jnp
from jax import lax
from jax.experimental import pallas as pl
from jax.experimental.pallas import tpu as pltpu
from jax.sharding import PartitionSpec as P

DELAYS = 8
MAXD = 12
LANES = 128
F32 = jnp.float32
BF16 = jnp.bfloat16


def passed_along(value, axis, steps):
    count = lax.axis_size(axis)
    first, last = (max(0, -steps), min(count, count - steps))
    return lax.ppermute(value, axis, [(source, source + steps) for source in range(first, last)])


def contract_rows(left, right):
    return lax.dot_general(
        left, right, (((0,), (0,)), ((), ())), preferred_element_type=jnp.float32
    )


def scaled_by(rotated, eigvals, ridge_grid, total_rows):
    penalty = 2.0 ** ((ridge_grid.astype(jnp.float32) - 8.0) * 0.5)
    scaled = rotated[None] / (
        math.sqrt(total_rows) * (eigvals[None, :, None] + penalty[:, None, None])
    )
    return scaled.astype(jnp.bfloat16)


def gathered(hidden, bold, panel, eigvals, ridge_grid, delays, runs):
    t_rows = hidden.shape[0]
    d_local = hidden.shape[1]
    v_cols = bold.shape[1]
    total_rows = t_rows * lax.axis_size("tm")
    first = lax.axis_index("tm") * t_rows
    ahead = passed_along(bold[:MAXD], "tm", -1)
    extended = jnp.concatenate([bold, ahead], 0)
    runs_pad = jnp.concatenate([runs, jnp.full((MAXD,), -1, jnp.int32)])
    own_runs = lax.dynamic_slice_in_dim(runs, first, t_rows)
    positions = first + jnp.arange(t_rows, dtype=jnp.int32)
    lagged_list = []
    for slot in range(DELAYS):
        offset = delays[slot]
        target_runs = lax.dynamic_slice_in_dim(runs_pad, first + offset, t_rows)
        valid = (positions + offset < total_rows) & (target_runs == own_runs)
        moved = lax.dynamic_slice_in_dim(extended, offset, t_rows, 0)
        lagged_list.append(jnp.where(valid[:, None], moved, jnp.zeros_like(moved)))
    stacked = jnp.stack(lagged_list, 1).reshape(t_rows, DELAYS * v_cols)
    cross = contract_rows(hidden, stacked)
    partial_cov = cross.reshape(d_local * DELAYS, v_cols).astype(jnp.bfloat16)
    panel_rows = lax.all_gather(panel, "tm", axis=0, tiled=True)
    rotated_part = contract_rows(
        lax.all_gather(panel_rows, "voxel", axis=1, tiled=True), partial_cov
    )
    rotated = lax.psum(rotated_part.astype(jnp.bfloat16), ("feature", "tm")).astype(jnp.float32)
    return scaled_by(rotated, eigvals, ridge_grid, total_rows)


def swapped(value, voxel, feature, tm):
    sizes = (lax.axis_size("voxel"), lax.axis_size("feature"), lax.axis_size("tm"))
    pairs = []
    for v in range(sizes[0]):
        for f in range(sizes[1]):
            for t in range(sizes[2]):
                source = (v * sizes[1] + f) * sizes[2] + t
                target = ((v ^ voxel) * sizes[1] + (f ^ feature)) * sizes[2] + (t ^ tm)
                pairs.append((source, target))
    return lax.ppermute(value, ("voxel", "feature", "tm"), pairs)


def sorted_by_slot(panel_t, sort, groups):
    rows = panel_t.shape[0]
    block = DELAYS * LANES
    stacked = jnp.concatenate([panel_t[:, g * block:(g + 1) * block] for g in range(groups)], 0)
    mixed = jnp.dot(stacked, sort[...], preferred_element_type=F32).astype(BF16)
    return [
        (k, g, mixed[g * rows:(g + 1) * rows, k * LANES:(k + 1) * LANES])
        for g in range(groups) for k in range(DELAYS)
    ]


def lag_sums(scalars, runs, products, total):
    p_cols = total.shape[0]
    tiles = products.shape[1] // LANES
    lane = lax.broadcasted_iota(jnp.int32, (8, LANES), 1)
    here = runs[...]
    kept = [(pltpu.roll(here, scalars[k], 1) == here).astype(F32) for k in range(DELAYS)]
    for row in range(0, p_cols, 8):
        sums = [total[row:row + 8, j * LANES:(j + 1) * LANES] for j in range(tiles)]
        for k in range(DELAYS):
            low = lane < scalars[k]
            before = jnp.zeros((8, LANES), F32)
            at = k * p_cols + row
            for j in range(tiles):
                if j < tiles - 1:
                    now = pltpu.roll(
                        products[at:at + 8, j * LANES:(j + 1) * LANES], scalars[k], 1
                    )
                    moved = jnp.where(low, before, now)
                    before = now
                else:
                    moved = jnp.where(low, before, 0.0)
                sums[j] = sums[j] + moved * kept[k][:, j * LANES:(j + 1) * LANES]
        for j in range(tiles):
            total[row:row + 8, j * LANES:(j + 1) * LANES] = sums[j]


def sort_into(ordered, panel_t, sort):
    rows = panel_t.shape[0]
    for k, g, tile in sorted_by_slot(panel_t, sort, ordered.shape[1] // LANES):
        ordered[k * rows:(k + 1) * rows, g * LANES:(g + 1) * LANES] = tile


def product(ordered, hidden):
    return lax.dot_general(
        ordered[...], hidden[...], (((1,), (1,)), ((), ())), preferred_element_type=F32
    )


def feature_copy(hidden, block, target, sem):
    width = target.shape[1]
    return pltpu.make_async_copy(
        hidden.at[:, pl.ds(pl.multiple_of(block * width, width), width)], target, sem
    )


def early_kernel(
    scalars, panel_t, panel_core, hidden, runs, total, sort, products, ordered, loaded, hidden_own, hidden_core, sems,
):
    rows = hidden.shape[0]
    tm = scalars[DELAYS]
    copies = [
        pltpu.make_async_copy(panel_t, loaded, sems.at[0]),
        feature_copy(hidden, tm, hidden_own, sems.at[1]),
        feature_copy(hidden, tm ^ 1, hidden_core, sems.at[2]),
    ]
    for copy in copies:
        copy.start()
    block = DELAYS * LANES
    gap = lax.broadcasted_iota(jnp.int32, (block, LANES), 0) - DELAYS * lax.broadcasted_iota(
        jnp.int32, (block, LANES), 1
    )
    for k in range(DELAYS):
        sort[:, k * LANES:(k + 1) * LANES] = (gap == k).astype(F32).astype(BF16)
    total[...] = jnp.zeros_like(total)
    copies[0].wait()
    sort_into(ordered, loaded[...], sort)
    copies[1].wait()
    products[:, :rows] = product(ordered, hidden_own)
    sort_into(ordered, panel_core[...], sort)
    copies[2].wait()
    products[:, :rows] += product(ordered, hidden_core)
    lag_sums(scalars, runs, products, total)


def own_kernel(panel_t, sort, hidden_own, products, ordered):
    sort_into(ordered, panel_t[...], sort)
    products[...] = product(ordered, hidden_own)


def late_kernel(
    scalars, panel_t, sort, hidden_core, own, runs, earlier, bold, bold_x, ahead, out, ordered, products, total,
):
    rows = hidden_core.shape[0]
    v_cols = bold.shape[1]
    total[...] = earlier[...]
    sort_into(ordered, panel_t[...], sort)
    products[:, :rows] = own[...] + product(ordered, hidden_core)
    lag_sums(scalars, runs, products, total)
    mine = total[:, :rows].astype(BF16)
    beyond = total[:, rows:].astype(BF16)
    blank = jnp.zeros((LANES - ahead.shape[0], v_cols), BF16)
    for place, part in enumerate((bold, bold_x)):
        out[:, place * v_cols:(place + 1) * v_cols] = jnp.dot(
            mine, part[...], preferred_element_type=F32
        ) + jnp.dot(
            beyond,
            jnp.concatenate([ahead[:, place * v_cols:(place + 1) * v_cols], blank], 0),
            preferred_element_type=F32,
        )


def head_kernel(bold, bold_x, head):
    v_cols = bold.shape[1]
    head[:, :v_cols] = bold[:16, :]
    head[:, v_cols:] = bold_x[:16, :]


def call(kernel, operands, out_shape, scratch, outside=()):
    hbm = pl.BlockSpec(memory_space=pltpu.HBM)
    operands = [
        pltpu.with_memory_space_constraint(operand, pltpu.HBM) if n in outside else operand
        for n, operand in enumerate(operands)
    ]
    vmem = pl.BlockSpec(memory_space=pltpu.VMEM)
    smem = pl.BlockSpec(memory_space=pltpu.SMEM)
    return pl.pallas_call(
        kernel,
        out_shape=out_shape,
        in_specs=[
            smem if operand.ndim == 1 else hbm if n in outside else vmem
            for n, operand in enumerate(operands)
        ],
        out_specs=jax.tree.map(lambda _: vmem, out_shape),
        scratch_shapes=scratch,
        compiler_params=pltpu.CompilerParams(vmem_limit_bytes=12 * 1024 * 1024),
        cost_estimate=pl.CostEstimate(flops=1024, bytes_accessed=1024, transcendentals=0),
    )(*operands)


def after(value, done):
    return lax.optimization_barrier((value, done))[0]


def exchanged(hidden, bold, panel, eigvals, ridge_grid, delays, runs):
    t_rows, d_local = hidden.shape
    v_cols = bold.shape[1]
    p_cols = panel.shape[1]
    tm_count = lax.axis_size("tm")
    total_rows = t_rows * tm_count
    width = d_local // tm_count
    block = DELAYS * LANES
    tm = lax.axis_index("tm")
    voxel = lax.axis_index("voxel")
    reach = t_rows + LANES
    dma = pltpu.SemaphoreType.DMA
    scalars = jnp.concatenate([delays, jnp.full((8,), tm, jnp.int32)])

    panel_t = panel.T
    late_t = swapped(panel_t, 0, 0, 2)

    bold_x = swapped(bold, 1, 0, 0)

    runs_pad = jnp.concatenate([runs, jnp.full((LANES,), -1, jnp.int32)])
    own_runs = lax.dynamic_slice_in_dim(runs_pad, tm * t_rows, reach)
    own_runs = jnp.broadcast_to(own_runs[None], (8, reach))
    panel_core = swapped(panel_t, 0, 0, 1)
    features = pltpu.VMEM((t_rows, width), BF16)
    ordered = pltpu.VMEM((DELAYS * p_cols, width), BF16)
    products = pltpu.VMEM((DELAYS * p_cols, reach), F32)
    earlier, sort = call(
        early_kernel, (scalars, panel_t, panel_core, hidden, own_runs),
        (jax.ShapeDtypeStruct((p_cols, reach), F32), jax.ShapeDtypeStruct((block, block), BF16)),
        [products, ordered, pltpu.VMEM(panel_t.shape, BF16), features, features, dma((3,))], (1, 3),
    )
    head = call(
        head_kernel, (bold, after(bold_x, earlier)),
        jax.ShapeDtypeStruct((16, 2 * v_cols), BF16), [],
    )
    ahead = passed_along(head, "tm", -1)
    hidden_late = after(hidden, head)
    hidden_own = lax.dynamic_slice_in_dim(hidden_late, (tm ^ 2) * width, width, 1)
    hidden_core = lax.dynamic_slice_in_dim(hidden_late, (tm ^ 3) * width, width, 1)
    late_t = after(late_t, (ahead, hidden_own, hidden_core))
    late_core = swapped(late_t, 0, 0, 1)
    own = call(
        own_kernel, (late_t, sort, hidden_own),
        jax.ShapeDtypeStruct((DELAYS * p_cols, t_rows), F32), [ordered],
    )
    part = call(
        late_kernel,
        (scalars, after(late_core, own), sort, hidden_core, own, own_runs, earlier, bold, bold_x, ahead),
        jax.ShapeDtypeStruct((p_cols, 2 * v_cols), F32),
        [ordered, products, pltpu.VMEM((p_cols, reach), F32)],
    )

    part = part + swapped(part.astype(BF16), 0, 0, 1).astype(F32)
    mine, theirs = part[:, :v_cols], part[:, v_cols:]
    mine_b, theirs_b = mine.astype(BF16), theirs.astype(BF16)
    from_y = swapped(mine_b, 0, 0, 2)
    from_x = swapped(theirs_b, 1, 0, 0)
    from_xy = swapped(theirs_b, 1, 0, 2)
    near = mine + from_y.astype(F32)
    far = from_x.astype(F32) + from_xy.astype(F32)
    rotated = jnp.where(
        voxel == 0, jnp.concatenate([near, far], 0), jnp.concatenate([far, near], 0)
    )
    rotated = rotated + swapped(rotated.astype(BF16), 0, 1, 0).astype(F32)
    rotated = rotated + swapped(rotated.astype(BF16), 0, 2, 0).astype(F32)
    return scaled_by(rotated, eigvals, ridge_grid, total_rows)


def solution(mesh):
    sizes = (mesh.shape["voxel"], mesh.shape["feature"], mesh.shape["tm"])
    shards = exchanged if sizes == (2, 4, 4) else gathered
    return jax.shard_map(
        shards,
        mesh=mesh,
        in_specs=(
            P("tm", "feature"),
            P("tm", "voxel"),
            P(("feature", "tm"), "voxel"),
            P(),
            P(),
            P(),
            P(),
        ),
        out_specs=P(None, None, "voxel"),
        check_vma=False,
    )
```

```python
import math

import jax
import jax.numpy as jnp
from jax import lax
from jax.experimental import pallas as pl
from jax.experimental.pallas import tpu as pltpu
from jax.sharding import PartitionSpec as P

DELAYS = 8
MAXD = 12
LANES = 128
F32 = jnp.float32
BF16 = jnp.bfloat16


def passed_along(value, axis, steps):
    count = lax.axis_size(axis)
    first, last = (max(0, -steps), min(count, count - steps))
    return lax.ppermute(value, axis, [(source, source + steps) for source in range(first, last)])


def contract_rows(left, right):
    return lax.dot_general(
        left, right, (((0,), (0,)), ((), ())), preferred_element_type=jnp.float32
    )


def scaled_by(rotated, eigvals, ridge_grid, total_rows):
    penalty = 2.0 ** ((ridge_grid.astype(jnp.float32) - 8.0) * 0.5)
    scaled = rotated[None] / (
        math.sqrt(total_rows) * (eigvals[None, :, None] + penalty[:, None, None])
    )
    return scaled.astype(jnp.bfloat16)


def gathered(hidden, bold, panel, eigvals, ridge_grid, delays, runs):
    t_rows = hidden.shape[0]
    d_local = hidden.shape[1]
    v_cols = bold.shape[1]
    total_rows = t_rows * lax.axis_size("tm")
    first = lax.axis_index("tm") * t_rows
    ahead = passed_along(bold[:MAXD], "tm", -1)
    extended = jnp.concatenate([bold, ahead], 0)
    runs_pad = jnp.concatenate([runs, jnp.full((MAXD,), -1, jnp.int32)])
    own_runs = lax.dynamic_slice_in_dim(runs, first, t_rows)
    positions = first + jnp.arange(t_rows, dtype=jnp.int32)
    lagged_list = []
    for slot in range(DELAYS):
        offset = delays[slot]
        target_runs = lax.dynamic_slice_in_dim(runs_pad, first + offset, t_rows)
        valid = (positions + offset < total_rows) & (target_runs == own_runs)
        moved = lax.dynamic_slice_in_dim(extended, offset, t_rows, 0)
        lagged_list.append(jnp.where(valid[:, None], moved, jnp.zeros_like(moved)))
    stacked = jnp.stack(lagged_list, 1).reshape(t_rows, DELAYS * v_cols)
    cross = contract_rows(hidden, stacked)
    partial_cov = cross.reshape(d_local * DELAYS, v_cols).astype(jnp.bfloat16)
    panel_rows = lax.all_gather(panel, "tm", axis=0, tiled=True)
    rotated_part = contract_rows(
        lax.all_gather(panel_rows, "voxel", axis=1, tiled=True), partial_cov
    )
    rotated = lax.psum(rotated_part.astype(jnp.bfloat16), ("feature", "tm")).astype(jnp.float32)
    return scaled_by(rotated, eigvals, ridge_grid, total_rows)


def swapped(value, voxel, feature, tm):
    sizes = (lax.axis_size("voxel"), lax.axis_size("feature"), lax.axis_size("tm"))
    pairs = []
    for v in range(sizes[0]):
        for f in range(sizes[1]):
            for t in range(sizes[2]):
                source = (v * sizes[1] + f) * sizes[2] + t
                target = ((v ^ voxel) * sizes[1] + (f ^ feature)) * sizes[2] + (t ^ tm)
                pairs.append((source, target))
    return lax.ppermute(value, ("voxel", "feature", "tm"), pairs)


def sort_matrices(sort):
    block = sort.shape[1]
    half = LANES // 2
    row = lax.broadcasted_iota(jnp.int32, (block, LANES), 0)
    lane = lax.broadcasted_iota(jnp.int32, (block, LANES), 1)
    upper = lane // half
    gap = row - DELAYS * (lane % half)
    for n, slot in enumerate((upper, 1 - upper)):
        for t in range(DELAYS // 2):
            sort[n, :, t * LANES:(t + 1) * LANES] = (gap - slot == 2 * t).astype(F32).astype(BF16)


def sort_into(ordered, panel_t, sort):
    rows = panel_t.shape[0]
    block = sort.shape[1]
    pairs = panel_t.shape[1] // (2 * block)
    mixed = [
        jnp.dot(
            jnp.concatenate(
                [panel_t[:, (2 * m + n) * block:(2 * m + n + 1) * block] for m in range(pairs)], 0
            ),
            sort[n], preferred_element_type=F32,
        )
        for n in range(2)
    ]
    low = lax.broadcasted_iota(jnp.int32, (rows, LANES), 1) < LANES // 2
    for m in range(pairs):
        for t in range(DELAYS // 2):
            first, second = (
                part[m * rows:(m + 1) * rows, t * LANES:(t + 1) * LANES] for part in mixed
            )
            for k, tile in (
                (2 * t, jnp.where(low, first, second)),
                (2 * t + 1, pltpu.roll(jnp.where(low, second, first), LANES // 2, 1)),
            ):
                ordered[k * rows:(k + 1) * rows, m * LANES:(m + 1) * LANES] = tile.astype(BF16)


def lag_sums(products, valid, first, shift, total, start):
    p_cols = total.shape[0]
    tiles = products.shape[1] // LANES
    places = valid.shape[0] // DELAYS
    stacked = []
    for j in range(tiles):
        parts = []
        for k in range(DELAYS):
            mask = jnp.broadcast_to(valid[pl.ds(k * places + first + j, 1), :], (p_cols, LANES))
            part = products[k * p_cols:(k + 1) * p_cols, j * LANES:(j + 1) * LANES]
            parts.append((part * mask).astype(BF16))
        stacked.append(jnp.concatenate(parts, 1))
    moved = jnp.dot(jnp.concatenate(stacked, 0), shift[...], preferred_element_type=F32)
    for j in range(tiles + 1):
        at = pl.ds(pl.multiple_of(start + j * LANES, LANES), LANES)
        add = total[:, at]
        if j < tiles:
            add = add + moved[j * p_cols:(j + 1) * p_cols, :LANES]
        if j > 0:
            add = add + moved[(j - 1) * p_cols:j * p_cols, LANES:]
        total[:, at] = add


def product(ordered, hidden):
    return lax.dot_general(
        ordered[...], hidden[...], (((1,), (1,)), ((), ())), preferred_element_type=F32
    )


def feature_copy(hidden, block, target, sem):
    width = target.shape[1]
    return pltpu.make_async_copy(
        hidden.at[:, pl.ds(pl.multiple_of(block * width, width), width)], target, sem
    )


def early_kernel(
    delays_in, panel_t, panel_core, hidden, runs, total, sort, valid, shift,
    delays, here, products, ordered, loaded, hidden_own, hidden_core, sems,
):
    rows = hidden.shape[0]
    tm = lax.axis_index("tm")
    copies = [
        pltpu.make_async_copy(delays_in, delays, sems.at[0]),
        pltpu.make_async_copy(runs, here, sems.at[1]),
        pltpu.make_async_copy(panel_t, loaded, sems.at[2]),
        feature_copy(hidden, tm, hidden_own, sems.at[3]),
        feature_copy(hidden, tm ^ 1, hidden_core, sems.at[4]),
    ]
    for copy in copies:
        copy.start()
    sort_matrices(sort)
    total[...] = jnp.zeros_like(total)
    copies[2].wait()
    sort_into(ordered, loaded[...], sort)
    copies[3].wait()
    products[...] = product(ordered, hidden_own)
    sort_into(ordered, panel_core[...], sort)
    copies[0].wait()
    copies[1].wait()
    places = here.shape[0]
    now = here[...]
    place = lax.broadcasted_iota(jnp.int32, now.shape, 0)
    lane = lax.broadcasted_iota(jnp.int32, now.shape, 1)
    later = jnp.where(place == places - 1, -1, pltpu.roll(now, places - 1, 0))
    row = lax.broadcasted_iota(jnp.int32, (LANES, 2 * LANES), 0)
    col = lax.broadcasted_iota(jnp.int32, (LANES, 2 * LANES), 1)
    for k in range(DELAYS):
        back = LANES - delays[k]
        target = jnp.where(lane < back, pltpu.roll(now, back, 1), pltpu.roll(later, back, 1))
        valid[k * places:(k + 1) * places, :] = (target == now).astype(F32)
        shift[k * LANES:(k + 1) * LANES, :] = (col - row == delays[k]).astype(F32).astype(BF16)
    copies[4].wait()
    products[...] += product(ordered, hidden_core)
    lag_sums(products, valid, tm * (rows // LANES), shift, total, 0)


def add_part(panel_t, sort, hidden, valid, shift, total, ordered, products):
    sort_into(ordered, panel_t[...], sort)
    products[...] = product(ordered, hidden)
    lag_sums(products, valid, lax.axis_index("tm") * (hidden.shape[0] // LANES), shift, total, 0)


def own_kernel(panel_t, sort, hidden, valid, shift, earlier, total, ordered, products):
    total[...] = earlier[...]
    add_part(panel_t, sort, hidden, valid, shift, total, ordered, products)


def late_kernel(
    panel_t, sort, hidden, valid, shift, earlier, bold, bold_x, ahead, out, ordered, products, total,
):
    rows, v_cols = bold.shape
    total[...] = earlier[...]
    add_part(panel_t, sort, hidden, valid, shift, total, ordered, products)
    mine = total[:, :rows].astype(BF16)
    beyond = total[:, rows:].astype(BF16)
    blank = jnp.zeros((LANES - ahead.shape[0], v_cols), BF16)
    for place, part in enumerate((bold, bold_x)):
        cols = slice(place * v_cols, (place + 1) * v_cols)
        out[:, cols] = jnp.dot(mine, part[...], preferred_element_type=F32) + jnp.dot(
            beyond, jnp.concatenate([ahead[:, cols], blank], 0), preferred_element_type=F32
        )


def head_kernel(bold, bold_x, head):
    v_cols = bold.shape[1]
    for place, part in enumerate((bold, bold_x)):
        head[:, place * v_cols:(place + 1) * v_cols] = part[:16, :]


def call(kernel, operands, out_shape, scratch, outside=()):
    hbm = pl.BlockSpec(memory_space=pltpu.HBM)
    operands = [
        pltpu.with_memory_space_constraint(operand, pltpu.HBM) if n in outside else operand
        for n, operand in enumerate(operands)
    ]
    vmem = pl.BlockSpec(memory_space=pltpu.VMEM)
    return pl.pallas_call(
        kernel,
        out_shape=out_shape,
        in_specs=[
            hbm if n in outside else vmem
            for n, operand in enumerate(operands)
        ],
        out_specs=jax.tree.map(lambda _: vmem, out_shape),
        scratch_shapes=scratch,
        compiler_params=pltpu.CompilerParams(vmem_limit_bytes=12 * 1024 * 1024),
        cost_estimate=pl.CostEstimate(flops=1024, bytes_accessed=1024, transcendentals=0),
    )(*operands)


def after(value, done):
    return lax.optimization_barrier((value, done))[0]


def exchanged(hidden, bold, panel, eigvals, ridge_grid, delays, runs):
    t_rows, d_local = hidden.shape
    v_cols = bold.shape[1]
    p_cols = panel.shape[1]
    tm_count = lax.axis_size("tm")
    total_rows = t_rows * tm_count
    width = d_local // tm_count
    block = DELAYS * LANES
    tm = lax.axis_index("tm")
    voxel = lax.axis_index("voxel")
    reach = t_rows + LANES
    dma = pltpu.SemaphoreType.DMA

    panel_t = panel.T
    late_t = swapped(panel_t, 0, 0, 2)
    panel_core = swapped(panel_t, 0, 0, 1)
    bold_x = swapped(bold, 1, 0, 0)

    places = runs.shape[0] // LANES
    features = pltpu.VMEM((t_rows, width), BF16)
    ordered = pltpu.VMEM((DELAYS * p_cols, width), BF16)
    products = pltpu.VMEM((DELAYS * p_cols, t_rows), F32)
    total = jax.ShapeDtypeStruct((p_cols, reach), F32)
    earlier, sort, valid, shift = call(
        early_kernel, (delays, panel_t, panel_core, hidden, runs.reshape(places, LANES)),
        (total, jax.ShapeDtypeStruct((2, block // 2, block // 2), BF16),
         jax.ShapeDtypeStruct((DELAYS * places, LANES), F32), jax.ShapeDtypeStruct((block, 2 * LANES), BF16)),
        [pltpu.SMEM(delays.shape, jnp.int32), pltpu.VMEM((places, LANES), jnp.int32),
         products, ordered, pltpu.VMEM(panel_t.shape, BF16), features, features, dma((5,))], (0, 1, 3, 4),
    )
    head = call(
        head_kernel, (bold, after(bold_x, earlier)), jax.ShapeDtypeStruct((16, 2 * v_cols), BF16), []
    )
    ahead = passed_along(head, "tm", -1)
    hidden_late = after(hidden, head)
    hidden_own = lax.dynamic_slice_in_dim(hidden_late, (tm ^ 2) * width, width, 1)
    hidden_core = lax.dynamic_slice_in_dim(hidden_late, (tm ^ 3) * width, width, 1)
    late_t = after(late_t, (ahead, hidden_own, hidden_core))
    late_core = swapped(late_t, 0, 0, 1)
    earlier = call(
        own_kernel, (late_t, sort, hidden_own, valid, shift, earlier), total, [ordered, products]
    )
    part = call(
        late_kernel,
        (after(late_core, earlier), sort, hidden_core, valid, shift, earlier, bold, bold_x, ahead),
        jax.ShapeDtypeStruct((p_cols, 2 * v_cols), F32),
        [ordered, products, pltpu.VMEM((p_cols, reach), F32)],
    )

    part = part + swapped(part.astype(BF16), 0, 0, 1).astype(F32)
    mine, theirs = part[:, :v_cols], part[:, v_cols:]
    mine_b, theirs_b = mine.astype(BF16), theirs.astype(BF16)
    from_y = swapped(mine_b, 0, 0, 2)
    from_x = swapped(theirs_b, 1, 0, 0)
    from_xy = swapped(theirs_b, 1, 0, 2)
    near = mine + from_y.astype(F32)
    far = from_x.astype(F32) + from_xy.astype(F32)
    rotated = jnp.where(
        voxel == 0, jnp.concatenate([near, far], 0), jnp.concatenate([far, near], 0)
    )
    rounded = rotated.astype(BF16)
    others = [swapped(rounded, 0, step, 0) for step in (1, 3, 2)]
    rotated = rotated + sum(other.astype(F32) for other in others)
    penalty = 2.0 ** ((ridge_grid.astype(F32) - 8.0) * 0.5)
    scale = 1.0 / (math.sqrt(total_rows) * (eigvals[None, :] + penalty[:, None]))
    return (rotated[None] * scale[:, :, None]).astype(BF16)


def solution(mesh):
    sizes = (mesh.shape["voxel"], mesh.shape["feature"], mesh.shape["tm"])
    shards = exchanged if sizes == (2, 4, 4) else gathered
    return jax.shard_map(
        shards,
        mesh=mesh,
        in_specs=(
            P("tm", "feature"),
            P("tm", "voxel"),
            P(("feature", "tm"), "voxel"),
            P(),
            P(),
            P(),
            P(),
        ),
        out_specs=P(None, None, "voxel"),
        check_vma=False,
    )
```

```python
import math

import jax
import jax.numpy as jnp
from jax import lax
from jax.experimental import pallas as pl
from jax.experimental.pallas import tpu as pltpu
from jax.sharding import PartitionSpec as P

DELAYS = 8
MAXD = 12
LANES = 128
F32 = jnp.float32
BF16 = jnp.bfloat16


def passed_along(value, axis, steps):
    count = lax.axis_size(axis)
    first, last = (max(0, -steps), min(count, count - steps))
    return lax.ppermute(value, axis, [(source, source + steps) for source in range(first, last)])


def contract_rows(left, right):
    return lax.dot_general(
        left, right, (((0,), (0,)), ((), ())), preferred_element_type=jnp.float32
    )


def scaled_by(rotated, eigvals, ridge_grid, total_rows):
    penalty = 2.0 ** ((ridge_grid.astype(jnp.float32) - 8.0) * 0.5)
    scaled = rotated[None] / (
        math.sqrt(total_rows) * (eigvals[None, :, None] + penalty[:, None, None])
    )
    return scaled.astype(jnp.bfloat16)


def gathered(hidden, bold, panel, eigvals, ridge_grid, delays, runs):
    t_rows = hidden.shape[0]
    d_local = hidden.shape[1]
    v_cols = bold.shape[1]
    total_rows = t_rows * lax.axis_size("tm")
    first = lax.axis_index("tm") * t_rows
    ahead = passed_along(bold[:MAXD], "tm", -1)
    extended = jnp.concatenate([bold, ahead], 0)
    runs_pad = jnp.concatenate([runs, jnp.full((MAXD,), -1, jnp.int32)])
    own_runs = lax.dynamic_slice_in_dim(runs, first, t_rows)
    positions = first + jnp.arange(t_rows, dtype=jnp.int32)
    lagged_list = []
    for slot in range(DELAYS):
        offset = delays[slot]
        target_runs = lax.dynamic_slice_in_dim(runs_pad, first + offset, t_rows)
        valid = (positions + offset < total_rows) & (target_runs == own_runs)
        moved = lax.dynamic_slice_in_dim(extended, offset, t_rows, 0)
        lagged_list.append(jnp.where(valid[:, None], moved, jnp.zeros_like(moved)))
    stacked = jnp.stack(lagged_list, 1).reshape(t_rows, DELAYS * v_cols)
    cross = contract_rows(hidden, stacked)
    partial_cov = cross.reshape(d_local * DELAYS, v_cols).astype(jnp.bfloat16)
    panel_rows = lax.all_gather(panel, "tm", axis=0, tiled=True)
    rotated_part = contract_rows(
        lax.all_gather(panel_rows, "voxel", axis=1, tiled=True), partial_cov
    )
    rotated = lax.psum(rotated_part.astype(jnp.bfloat16), ("feature", "tm")).astype(jnp.float32)
    return scaled_by(rotated, eigvals, ridge_grid, total_rows)


def swapped(value, voxel, feature, tm):
    sizes = (lax.axis_size("voxel"), lax.axis_size("feature"), lax.axis_size("tm"))
    pairs = []
    for v in range(sizes[0]):
        for f in range(sizes[1]):
            for t in range(sizes[2]):
                source = (v * sizes[1] + f) * sizes[2] + t
                target = ((v ^ voxel) * sizes[1] + (f ^ feature)) * sizes[2] + (t ^ tm)
                pairs.append((source, target))
    return lax.ppermute(value, ("voxel", "feature", "tm"), pairs)


GROUPS = 4


def sort_matrices(sort):
    width = LANES // GROUPS
    row = lax.broadcasted_iota(jnp.int32, (sort.shape[1], LANES), 0)
    lane = lax.broadcasted_iota(jnp.int32, (sort.shape[1], LANES), 1)
    gap = row - DELAYS * (lane % width)
    for n in range(GROUPS):
        slot = (lane // width - n) % GROUPS
        for t in range(DELAYS // GROUPS):
            sort[n, :, t * LANES:(t + 1) * LANES] = (gap - slot == GROUPS * t).astype(F32).astype(BF16)


def sort_into(ordered, panel_t, sort):
    rows = panel_t.shape[0]
    block = sort.shape[1]
    width = LANES // GROUPS
    tiles = panel_t.shape[1] // (GROUPS * block)
    mixed = [
        jnp.dot(
            jnp.concatenate(
                [panel_t[:, (GROUPS * m + n) * block:(GROUPS * m + n + 1) * block] for m in range(tiles)], 0
            ),
            sort[n], preferred_element_type=F32,
        )
        for n in range(GROUPS)
    ]
    lane = lax.broadcasted_iota(jnp.int32, (rows, LANES), 1)
    for m in range(tiles):
        for t in range(DELAYS // GROUPS):
            parts = [part[m * rows:(m + 1) * rows, t * LANES:(t + 1) * LANES] for part in mixed]
            for r in range(GROUPS):
                tile = parts[(GROUPS - 1 - r) % GROUPS]
                for place in range(GROUPS - 2, -1, -1):
                    tile = jnp.where(lane < (place + 1) * width, parts[(place - r) % GROUPS], tile)
                if r:
                    tile = pltpu.roll(tile, LANES - r * width, 1)
                k = t * GROUPS + r
                ordered[k * rows:(k + 1) * rows, m * LANES:(m + 1) * LANES] = tile.astype(BF16)


def lag_sums(products, valid, shift, total):
    p_cols = total.shape[0]
    tiles = products.shape[1] // LANES
    places = valid.shape[0] // DELAYS
    stacked = []
    for j in range(tiles):
        parts = []
        for k in range(DELAYS):
            mask = valid[k * places + j:k * places + j + 1, :]
            part = products[k * p_cols:(k + 1) * p_cols, j * LANES:(j + 1) * LANES]
            parts.append((part * mask).astype(BF16))
        stacked.append(jnp.concatenate(parts, 1))
    moved = jnp.dot(jnp.concatenate(stacked, 0), shift[...], preferred_element_type=F32)
    for j in range(tiles + 1):
        at = slice(j * LANES, (j + 1) * LANES)
        add = total[:, at]
        if j < tiles:
            add = add + moved[j * p_cols:(j + 1) * p_cols, :LANES]
        if j > 0:
            add = add + moved[(j - 1) * p_cols:j * p_cols, LANES:]
        total[:, at] = add


def product(ordered, hidden):
    return lax.dot_general(
        ordered[...], hidden[...], (((1,), (1,)), ((), ())), preferred_element_type=F32
    )


def feature_copy(hidden, block, target, sem):
    width = target.shape[1]
    return pltpu.make_async_copy(
        hidden.at[:, pl.ds(pl.multiple_of(block * width, width), width)], target, sem
    )


def early_kernel(
    delays_in, panel_t, panel_core, hidden, runs, total, sort, valid, shift,
    delays, here, all_valid, products, ordered, loaded, hidden_own, hidden_core, sems,
):
    rows = hidden.shape[0]
    tiles, kept = rows // LANES, valid.shape[0] // DELAYS
    tm = lax.axis_index("tm")
    copies = [
        pltpu.make_async_copy(delays_in, delays, sems.at[0]),
        pltpu.make_async_copy(runs, here, sems.at[1]),
        pltpu.make_async_copy(panel_t, loaded, sems.at[2]),
        feature_copy(hidden, tm, hidden_own, sems.at[3]),
        feature_copy(hidden, tm ^ 1, hidden_core, sems.at[4]),
    ]
    for copy in copies:
        copy.start()
    sort_matrices(sort)
    total[...] = jnp.zeros_like(total)
    copies[2].wait()
    sort_into(ordered, loaded[...], sort)
    copies[3].wait()
    products[...] = product(ordered, hidden_own)
    sort_into(ordered, panel_core[...], sort)
    copies[0].wait()
    copies[1].wait()
    places = here.shape[0]
    now = here[...]
    place = lax.broadcasted_iota(jnp.int32, now.shape, 0)
    lane = lax.broadcasted_iota(jnp.int32, now.shape, 1)
    later = jnp.where(place == places - 1, -1, pltpu.roll(now, places - 1, 0))
    row = lax.broadcasted_iota(jnp.int32, (LANES, 2 * LANES), 0)
    col = lax.broadcasted_iota(jnp.int32, (LANES, 2 * LANES), 1)
    for k in range(DELAYS):
        back = LANES - delays[k]
        target = jnp.where(lane < back, pltpu.roll(now, back, 1), pltpu.roll(later, back, 1))
        all_valid[k * places:(k + 1) * places, :] = (target == now).astype(F32)
        valid[k * kept:k * kept + tiles, :] = all_valid[pl.ds(k * places + tm * tiles, tiles), :]
        shift[k * LANES:(k + 1) * LANES, :] = (col - row == delays[k]).astype(F32).astype(BF16)
    copies[4].wait()
    products[...] += product(ordered, hidden_core)
    lag_sums(products, valid, shift, total)


def add_part(panel_t, sort, hidden, valid, shift, total, ordered, products):
    sort_into(ordered, panel_t[...], sort)
    products[...] = product(ordered, hidden)
    lag_sums(products, valid, shift, total)


def own_kernel(panel_t, sort, hidden, valid, shift, earlier, total, ordered, products):
    total[...] = earlier[...]
    add_part(panel_t, sort, hidden, valid, shift, total, ordered, products)


def late_kernel(
    panel_t, sort, hidden, valid, shift, earlier, bold, bold_x, ahead, out, ordered, products, total,
):
    rows, v_cols = bold.shape
    total[...] = earlier[...]
    add_part(panel_t, sort, hidden, valid, shift, total, ordered, products)
    mine = total[:, :rows].astype(BF16)
    beyond = total[:, rows:].astype(BF16)
    blank = jnp.zeros((LANES - ahead.shape[0], v_cols), BF16)
    for place, part in enumerate((bold, bold_x)):
        cols = slice(place * v_cols, (place + 1) * v_cols)
        out[:, cols] = jnp.dot(mine, part[...], preferred_element_type=F32) + jnp.dot(
            beyond, jnp.concatenate([ahead[:, cols], blank], 0), preferred_element_type=F32
        )


def head_kernel(bold, bold_x, head):
    v_cols = bold.shape[1]
    for place, part in enumerate((bold, bold_x)):
        head[:, place * v_cols:(place + 1) * v_cols] = part[:16, :]


PARTS = 8


def scale_kernel(rotated, scale, out, scaled, sems):
    step = scaled.shape[0] // PARTS
    total = rotated[...]
    copies = []
    for part in range(PARTS):
        for r in range(part * step, (part + 1) * step):
            scaled[r] = (total * scale[r]).astype(BF16)
        rows = pl.ds(part * step, step)
        copies.append(pltpu.make_async_copy(scaled.at[rows], out.at[rows], sems.at[part]))
        copies[-1].start()
    for copy in copies:
        copy.wait()


def call(kernel, operands, out_shape, scratch, outside=()):
    hbm = pl.BlockSpec(memory_space=pltpu.HBM)
    operands = [
        pltpu.with_memory_space_constraint(operand, pltpu.HBM) if n in outside else operand
        for n, operand in enumerate(operands)
    ]
    vmem = pl.BlockSpec(memory_space=pltpu.VMEM)
    return pl.pallas_call(
        kernel,
        out_shape=out_shape,
        in_specs=[
            hbm if n in outside else vmem
            for n, operand in enumerate(operands)
        ],
        out_specs=jax.tree.map(lambda _: vmem, out_shape),
        scratch_shapes=scratch,
        compiler_params=pltpu.CompilerParams(vmem_limit_bytes=12 * 1024 * 1024),
        cost_estimate=pl.CostEstimate(flops=1024, bytes_accessed=1024, transcendentals=0),
    )(*operands)


def after(value, done):
    return lax.optimization_barrier((value, done))[0]


def exchanged(hidden, bold, panel, eigvals, ridge_grid, delays, runs):
    t_rows, d_local = hidden.shape
    v_cols = bold.shape[1]
    p_cols = panel.shape[1]
    tm_count = lax.axis_size("tm")
    total_rows = t_rows * tm_count
    width = d_local // tm_count
    block = DELAYS * LANES
    tm = lax.axis_index("tm")
    voxel = lax.axis_index("voxel")
    reach = t_rows + LANES
    dma = pltpu.SemaphoreType.DMA

    panel_t = panel.T
    late_t = swapped(panel_t, 0, 0, 2)
    panel_core = swapped(panel_t, 0, 0, 1)
    bold_x = swapped(bold, 1, 0, 0)

    places = runs.shape[0] // LANES
    features = pltpu.VMEM((t_rows, width), BF16)
    ordered = pltpu.VMEM((DELAYS * p_cols, width), BF16)
    products = pltpu.VMEM((DELAYS * p_cols, t_rows), F32)
    total = jax.ShapeDtypeStruct((p_cols, reach), F32)
    earlier, sort, valid, shift = call(
        early_kernel, (delays, panel_t, panel_core, hidden, runs.reshape(places, LANES)),
        (total, jax.ShapeDtypeStruct((GROUPS, block // GROUPS, block // GROUPS), BF16),
         jax.ShapeDtypeStruct((DELAYS * -(-t_rows // (8 * LANES)) * 8, LANES), F32), jax.ShapeDtypeStruct((block, 2 * LANES), BF16)),
        [pltpu.SMEM(delays.shape, jnp.int32), pltpu.VMEM((places, LANES), jnp.int32),
         pltpu.VMEM((DELAYS * places, LANES), F32),
         products, ordered, pltpu.VMEM(panel_t.shape, BF16), features, features, dma((5,))], (0, 1, 3, 4),
    )
    penalty = 2.0 ** ((ridge_grid.astype(F32) - 8.0) * 0.5)
    scale = 1.0 / (math.sqrt(total_rows) * (eigvals[None, :] + penalty[:, None]))
    scale = jnp.broadcast_to(scale[:, :, None], (*scale.shape, v_cols))
    head = call(
        head_kernel, (bold, after(bold_x, (earlier, scale))), jax.ShapeDtypeStruct((16, 2 * v_cols), BF16), []
    )
    ahead = passed_along(head, "tm", -1)
    hidden_late = after(hidden, head)
    hidden_own = lax.dynamic_slice_in_dim(hidden_late, (tm ^ 2) * width, width, 1)
    hidden_core = lax.dynamic_slice_in_dim(hidden_late, (tm ^ 3) * width, width, 1)
    late_t = after(late_t, (ahead, hidden_own, hidden_core))
    late_core = swapped(late_t, 0, 0, 1)
    earlier = call(
        own_kernel, (late_t, sort, hidden_own, valid, shift, earlier), total, [ordered, products]
    )
    part = call(
        late_kernel,
        (after(late_core, earlier), sort, hidden_core, valid, shift, earlier, bold, bold_x, ahead),
        jax.ShapeDtypeStruct((p_cols, 2 * v_cols), F32),
        [ordered, products, pltpu.VMEM((p_cols, reach), F32)],
    )

    part = part + swapped(part.astype(BF16), 0, 0, 1).astype(F32)
    mine, theirs = part[:, :v_cols], part[:, v_cols:]
    mine_b, theirs_b = mine.astype(BF16), theirs.astype(BF16)
    from_y = swapped(mine_b, 0, 0, 2)
    from_x = swapped(theirs_b, 1, 0, 0)
    from_xy = swapped(theirs_b, 1, 0, 2)
    near = mine + from_y.astype(F32)
    far = from_x.astype(F32) + from_xy.astype(F32)
    rotated = jnp.where(
        voxel == 0, jnp.concatenate([near, far], 0), jnp.concatenate([far, near], 0)
    )
    rounded = rotated.astype(BF16)
    others = [swapped(rounded, 0, step, 0) for step in (1, 3, 2)]
    rotated = rotated + sum(other.astype(F32) for other in others)
    shape = (ridge_grid.shape[0], 2 * p_cols, v_cols)
    return pl.pallas_call(
        scale_kernel,
        out_shape=jax.ShapeDtypeStruct(shape, BF16),
        in_specs=2 * [pl.BlockSpec(memory_space=pltpu.VMEM)],
        out_specs=pl.BlockSpec(memory_space=pl.ANY),
        scratch_shapes=[pltpu.VMEM(shape, BF16), dma((PARTS,))],
        compiler_params=pltpu.CompilerParams(vmem_limit_bytes=4 * 1024 * 1024),
    )(rotated, scale)


def solution(mesh):
    sizes = (mesh.shape["voxel"], mesh.shape["feature"], mesh.shape["tm"])
    shards = exchanged if sizes == (2, 4, 4) else gathered
    return jax.shard_map(
        shards,
        mesh=mesh,
        in_specs=(
            P("tm", "feature"),
            P("tm", "voxel"),
            P(("feature", "tm"), "voxel"),
            P(),
            P(),
            P(),
            P(),
        ),
        out_specs=P(None, None, "voxel"),
        check_vma=False,
    )
```

```python
import math

import jax
import jax.numpy as jnp
from jax import lax
from jax.experimental import pallas as pl
from jax.experimental.pallas import tpu as pltpu
from jax.sharding import PartitionSpec as P

DELAYS = 8
MAXD = 12
LANES = 128
F32 = jnp.float32
BF16 = jnp.bfloat16


def passed_along(value, axis, steps):
    count = lax.axis_size(axis)
    first, last = (max(0, -steps), min(count, count - steps))
    return lax.ppermute(value, axis, [(source, source + steps) for source in range(first, last)])


def contract_rows(left, right):
    return lax.dot_general(
        left, right, (((0,), (0,)), ((), ())), preferred_element_type=jnp.float32
    )


def scaled_by(rotated, eigvals, ridge_grid, total_rows):
    penalty = 2.0 ** ((ridge_grid.astype(jnp.float32) - 8.0) * 0.5)
    scaled = rotated[None] / (
        math.sqrt(total_rows) * (eigvals[None, :, None] + penalty[:, None, None])
    )
    return scaled.astype(jnp.bfloat16)


def gathered(hidden, bold, panel, eigvals, ridge_grid, delays, runs):
    t_rows = hidden.shape[0]
    d_local = hidden.shape[1]
    v_cols = bold.shape[1]
    total_rows = t_rows * lax.axis_size("tm")
    first = lax.axis_index("tm") * t_rows
    ahead = passed_along(bold[:MAXD], "tm", -1)
    extended = jnp.concatenate([bold, ahead], 0)
    runs_pad = jnp.concatenate([runs, jnp.full((MAXD,), -1, jnp.int32)])
    own_runs = lax.dynamic_slice_in_dim(runs, first, t_rows)
    positions = first + jnp.arange(t_rows, dtype=jnp.int32)
    lagged_list = []
    for slot in range(DELAYS):
        offset = delays[slot]
        target_runs = lax.dynamic_slice_in_dim(runs_pad, first + offset, t_rows)
        valid = (positions + offset < total_rows) & (target_runs == own_runs)
        moved = lax.dynamic_slice_in_dim(extended, offset, t_rows, 0)
        lagged_list.append(jnp.where(valid[:, None], moved, jnp.zeros_like(moved)))
    stacked = jnp.stack(lagged_list, 1).reshape(t_rows, DELAYS * v_cols)
    cross = contract_rows(hidden, stacked)
    partial_cov = cross.reshape(d_local * DELAYS, v_cols).astype(jnp.bfloat16)
    panel_rows = lax.all_gather(panel, "tm", axis=0, tiled=True)
    rotated_part = contract_rows(
        lax.all_gather(panel_rows, "voxel", axis=1, tiled=True), partial_cov
    )
    rotated = lax.psum(rotated_part.astype(jnp.bfloat16), ("feature", "tm")).astype(jnp.float32)
    return scaled_by(rotated, eigvals, ridge_grid, total_rows)


def swapped(value, voxel, feature, tm):
    sizes = (lax.axis_size("voxel"), lax.axis_size("feature"), lax.axis_size("tm"))
    pairs = []
    for v in range(sizes[0]):
        for f in range(sizes[1]):
            for t in range(sizes[2]):
                source = (v * sizes[1] + f) * sizes[2] + t
                target = ((v ^ voxel) * sizes[1] + (f ^ feature)) * sizes[2] + (t ^ tm)
                pairs.append((source, target))
    return lax.ppermute(value, ("voxel", "feature", "tm"), pairs)


GROUPS = 4


def sort_matrices(sort):
    width = LANES // GROUPS
    row = lax.broadcasted_iota(jnp.int32, (sort.shape[1], LANES), 0)
    lane = lax.broadcasted_iota(jnp.int32, (sort.shape[1], LANES), 1)
    gap = row - DELAYS * (lane % width)
    for n in range(GROUPS):
        slot = (lane // width - n) % GROUPS
        for t in range(DELAYS // GROUPS):
            sort[n, :, t * LANES:(t + 1) * LANES] = (gap - slot == GROUPS * t).astype(F32).astype(BF16)


def sort_into(ordered, panel_t, sort):
    rows = panel_t.shape[0]
    block = sort.shape[1]
    width = LANES // GROUPS
    tiles = panel_t.shape[1] // (GROUPS * block)
    mixed = [
        jnp.dot(
            jnp.concatenate(
                [panel_t[:, (GROUPS * m + n) * block:(GROUPS * m + n + 1) * block] for m in range(tiles)], 0
            ),
            sort[n], preferred_element_type=F32,
        )
        for n in range(GROUPS)
    ]
    lane = lax.broadcasted_iota(jnp.int32, (rows, LANES), 1)
    for m in range(tiles):
        for t in range(DELAYS // GROUPS):
            parts = [part[m * rows:(m + 1) * rows, t * LANES:(t + 1) * LANES] for part in mixed]
            for r in range(GROUPS):
                tile = parts[(GROUPS - 1 - r) % GROUPS]
                for place in range(GROUPS - 2, -1, -1):
                    tile = jnp.where(lane < (place + 1) * width, parts[(place - r) % GROUPS], tile)
                if r:
                    tile = pltpu.roll(tile, LANES - r * width, 1)
                k = t * GROUPS + r
                ordered[k * rows:(k + 1) * rows, m * LANES:(m + 1) * LANES] = tile.astype(BF16)


def lag_sums(products, valid, shift, total):
    p_cols = total.shape[0]
    tiles = products.shape[1] // LANES
    places = valid.shape[0] // DELAYS
    stacked = []
    for j in range(tiles):
        parts = []
        for k in range(DELAYS):
            mask = valid[k * places + j:k * places + j + 1, :]
            part = products[k * p_cols:(k + 1) * p_cols, j * LANES:(j + 1) * LANES]
            parts.append((part * mask).astype(BF16))
        stacked.append(jnp.concatenate(parts, 1))
    moved = jnp.dot(jnp.concatenate(stacked, 0), shift[...], preferred_element_type=F32)
    for j in range(tiles + 1):
        at = slice(j * LANES, (j + 1) * LANES)
        add = total[:, at]
        if j < tiles:
            add = add + moved[j * p_cols:(j + 1) * p_cols, :LANES]
        if j > 0:
            add = add + moved[(j - 1) * p_cols:j * p_cols, LANES:]
        total[:, at] = add


def product(ordered, hidden):
    return lax.dot_general(
        ordered[...], hidden[...], (((1,), (1,)), ((), ())), preferred_element_type=F32
    )


def feature_copy(hidden, block, target, sem):
    width = target.shape[1]
    return pltpu.make_async_copy(
        hidden.at[:, pl.ds(pl.multiple_of(block * width, width), width)], target, sem
    )


def early_kernel(
    delays_in, panel_t, panel_core, hidden, runs, total, sort, valid, shift,
    delays, here, all_valid, products, ordered, loaded, hidden_own, hidden_core, sems,
):
    rows = hidden.shape[0]
    tiles, kept = rows // LANES, valid.shape[0] // DELAYS
    tm = lax.axis_index("tm")
    copies = [
        pltpu.make_async_copy(delays_in, delays, sems.at[0]),
        pltpu.make_async_copy(runs, here, sems.at[1]),
        pltpu.make_async_copy(panel_t, loaded, sems.at[2]),
        feature_copy(hidden, tm, hidden_own, sems.at[3]),
        feature_copy(hidden, tm ^ 1, hidden_core, sems.at[4]),
    ]
    for copy in copies:
        copy.start()
    sort_matrices(sort)
    total[...] = jnp.zeros_like(total)
    copies[2].wait()
    sort_into(ordered, loaded[...], sort)
    copies[3].wait()
    products[...] = product(ordered, hidden_own)
    sort_into(ordered, panel_core[...], sort)
    copies[0].wait()
    copies[1].wait()
    places = here.shape[0]
    now = here[...]
    place = lax.broadcasted_iota(jnp.int32, now.shape, 0)
    lane = lax.broadcasted_iota(jnp.int32, now.shape, 1)
    later = jnp.where(place == places - 1, -1, pltpu.roll(now, places - 1, 0))
    row = lax.broadcasted_iota(jnp.int32, (LANES, 2 * LANES), 0)
    col = lax.broadcasted_iota(jnp.int32, (LANES, 2 * LANES), 1)
    for k in range(DELAYS):
        back = LANES - delays[k]
        target = jnp.where(lane < back, pltpu.roll(now, back, 1), pltpu.roll(later, back, 1))
        all_valid[k * places:(k + 1) * places, :] = (target == now).astype(F32)
        valid[k * kept:k * kept + tiles, :] = all_valid[pl.ds(k * places + tm * tiles, tiles), :]
        shift[k * LANES:(k + 1) * LANES, :] = (col - row == delays[k]).astype(F32).astype(BF16)
    copies[4].wait()
    products[...] += product(ordered, hidden_core)
    lag_sums(products, valid, shift, total)


def add_part(panel_t, sort, hidden, valid, shift, total, ordered, products):
    sort_into(ordered, panel_t[...], sort)
    products[...] = product(ordered, hidden)
    lag_sums(products, valid, shift, total)


def own_kernel(panel_t, sort, hidden, valid, shift, earlier, total, ordered, products):
    total[...] = earlier[...]
    add_part(panel_t, sort, hidden, valid, shift, total, ordered, products)


def late_kernel(
    panel_t, sort, hidden, valid, shift, earlier, bold, bold_x, ahead, out, ordered, products, total,
):
    rows, v_cols = bold.shape
    total[...] = earlier[...]
    add_part(panel_t, sort, hidden, valid, shift, total, ordered, products)
    mine = total[:, :rows].astype(BF16)
    beyond = total[:, rows:].astype(BF16)
    blank = jnp.zeros((LANES - ahead.shape[0], v_cols), BF16)
    for place, part in enumerate((bold, bold_x)):
        cols = slice(place * v_cols, (place + 1) * v_cols)
        out[:, cols] = jnp.dot(mine, part[...], preferred_element_type=F32) + jnp.dot(
            beyond, jnp.concatenate([ahead[:, cols], blank], 0), preferred_element_type=F32
        )


def head_kernel(bold, bold_x, head):
    v_cols = bold.shape[1]
    for place, part in enumerate((bold, bold_x)):
        head[:, place * v_cols:(place + 1) * v_cols] = part[:16, :]


PARTS = 8


def scale_kernel(rotated, scale, out, scaled, sems):
    step = scaled.shape[0] // PARTS
    total = rotated[...]
    copies = []
    for part in range(PARTS):
        for r in range(part * step, (part + 1) * step):
            scaled[r] = (total * scale[r]).astype(BF16)
        rows = pl.ds(part * step, step)
        copies.append(pltpu.make_async_copy(scaled.at[rows], out.at[rows], sems.at[part]))
        copies[-1].start()
    for copy in copies:
        copy.wait()


def call(kernel, operands, out_shape, scratch, outside=()):
    hbm = pl.BlockSpec(memory_space=pltpu.HBM)
    operands = [
        pltpu.with_memory_space_constraint(operand, pltpu.HBM) if n in outside else operand
        for n, operand in enumerate(operands)
    ]
    vmem = pl.BlockSpec(memory_space=pltpu.VMEM)
    return pl.pallas_call(
        kernel,
        out_shape=out_shape,
        in_specs=[
            hbm if n in outside else vmem
            for n, operand in enumerate(operands)
        ],
        out_specs=jax.tree.map(lambda _: vmem, out_shape),
        scratch_shapes=scratch,
        compiler_params=pltpu.CompilerParams(vmem_limit_bytes=12 * 1024 * 1024),
        cost_estimate=pl.CostEstimate(flops=1024, bytes_accessed=1024, transcendentals=0),
    )(*operands)


def after(value, done):
    return lax.optimization_barrier((value, done))[0]


def exchanged(hidden, bold, panel, eigvals, ridge_grid, delays, runs):
    t_rows, d_local = hidden.shape
    v_cols = bold.shape[1]
    p_cols = panel.shape[1]
    tm_count = lax.axis_size("tm")
    total_rows = t_rows * tm_count
    width = d_local // tm_count
    block = DELAYS * LANES
    tm = lax.axis_index("tm")
    voxel = lax.axis_index("voxel")
    reach = t_rows + LANES
    dma = pltpu.SemaphoreType.DMA

    panel_t = panel.T
    late_t = swapped(panel_t, 0, 0, 2)
    panel_core = swapped(panel_t, 0, 0, 1)
    bold_x = swapped(bold, 1, 0, 0)

    places = runs.shape[0] // LANES
    features = pltpu.VMEM((t_rows, width), BF16)
    ordered = pltpu.VMEM((DELAYS * p_cols, width), BF16)
    products = pltpu.VMEM((DELAYS * p_cols, t_rows), F32)
    total = jax.ShapeDtypeStruct((p_cols, reach), F32)
    earlier, sort, valid, shift = call(
        early_kernel, (delays, panel_t, panel_core, hidden, runs.reshape(places, LANES)),
        (total, jax.ShapeDtypeStruct((GROUPS, block // GROUPS, block // GROUPS), BF16),
         jax.ShapeDtypeStruct((DELAYS * -(-t_rows // (8 * LANES)) * 8, LANES), F32), jax.ShapeDtypeStruct((block, 2 * LANES), BF16)),
        [pltpu.SMEM(delays.shape, jnp.int32), pltpu.VMEM((places, LANES), jnp.int32),
         pltpu.VMEM((DELAYS * places, LANES), F32),
         products, ordered, pltpu.VMEM(panel_t.shape, BF16), features, features, dma((5,))], (0, 1, 3, 4),
    )
    penalty = 2.0 ** ((ridge_grid.astype(F32) - 8.0) * 0.5)
    scale = 1.0 / (math.sqrt(total_rows) * (eigvals[None, :] + penalty[:, None]))
    scale = jnp.broadcast_to(scale[:, :, None], (*scale.shape, v_cols))
    head = call(
        head_kernel, (bold, after(bold_x, (earlier, scale))), jax.ShapeDtypeStruct((16, 2 * v_cols), BF16), []
    )
    ahead = passed_along(head, "tm", -1)
    hidden_late = after(hidden, head)
    hidden_own = lax.dynamic_slice_in_dim(hidden_late, (tm ^ 2) * width, width, 1)
    hidden_core = lax.dynamic_slice_in_dim(hidden_late, (tm ^ 3) * width, width, 1)
    late_t = after(late_t, (ahead, hidden_own, hidden_core))
    late_core = swapped(late_t, 0, 0, 1)
    earlier = call(
        own_kernel, (late_t, sort, hidden_own, valid, shift, earlier), total, [ordered, products]
    )
    part = call(
        late_kernel,
        (after(late_core, earlier), sort, hidden_core, valid, shift, earlier, bold, bold_x, ahead),
        jax.ShapeDtypeStruct((p_cols, 2 * v_cols), F32),
        [ordered, products, pltpu.VMEM((p_cols, reach), F32)],
    )

    part = part.astype(BF16)
    part = part.astype(F32) + swapped(part, 0, 0, 1).astype(F32)
    mine, theirs = part[:, :v_cols].astype(BF16), part[:, v_cols:].astype(BF16)
    from_y = swapped(mine, 0, 0, 3)
    from_x = swapped(theirs, 1, 0, 1)
    from_xy = swapped(theirs, 1, 0, 3)
    near = mine.astype(F32) + from_y.astype(F32)
    far = from_x.astype(F32) + from_xy.astype(F32)
    rotated = jnp.where(
        voxel == 0, jnp.concatenate([near, far], 0), jnp.concatenate([far, near], 0)
    )
    for step in (1, 2):
        rounded = rotated.astype(BF16)
        rotated = rounded.astype(F32) + swapped(rounded, 0, step, 1).astype(F32)
    shape = (ridge_grid.shape[0], 2 * p_cols, v_cols)
    return pl.pallas_call(
        scale_kernel,
        out_shape=jax.ShapeDtypeStruct(shape, BF16),
        in_specs=2 * [pl.BlockSpec(memory_space=pltpu.VMEM)],
        out_specs=pl.BlockSpec(memory_space=pl.ANY),
        scratch_shapes=[pltpu.VMEM(shape, BF16), dma((PARTS,))],
        compiler_params=pltpu.CompilerParams(vmem_limit_bytes=4 * 1024 * 1024),
    )(rotated, scale)


def solution(mesh):
    sizes = (mesh.shape["voxel"], mesh.shape["feature"], mesh.shape["tm"])
    shards = exchanged if sizes == (2, 4, 4) else gathered
    return jax.shard_map(
        shards,
        mesh=mesh,
        in_specs=(
            P("tm", "feature"),
            P("tm", "voxel"),
            P(("feature", "tm"), "voxel"),
            P(),
            P(),
            P(),
            P(),
        ),
        out_specs=P(None, None, "voxel"),
        check_vma=False,
    )
```

```python
import math

import jax
import jax.numpy as jnp
from jax import lax
from jax.experimental import pallas as pl
from jax.experimental.pallas import tpu as pltpu
from jax.sharding import PartitionSpec as P

DELAYS = 8
MAXD = 12
LANES = 128
F32 = jnp.float32
BF16 = jnp.bfloat16


def passed_along(value, axis, steps):
    count = lax.axis_size(axis)
    first, last = (max(0, -steps), min(count, count - steps))
    return lax.ppermute(value, axis, [(source, source + steps) for source in range(first, last)])


def contract_rows(left, right):
    return lax.dot_general(
        left, right, (((0,), (0,)), ((), ())), preferred_element_type=jnp.float32
    )


def scaled_by(rotated, eigvals, ridge_grid, total_rows):
    penalty = 2.0 ** ((ridge_grid.astype(jnp.float32) - 8.0) * 0.5)
    scaled = rotated[None] / (
        math.sqrt(total_rows) * (eigvals[None, :, None] + penalty[:, None, None])
    )
    return scaled.astype(jnp.bfloat16)


def gathered(hidden, bold, panel, eigvals, ridge_grid, delays, runs):
    t_rows = hidden.shape[0]
    d_local = hidden.shape[1]
    v_cols = bold.shape[1]
    total_rows = t_rows * lax.axis_size("tm")
    first = lax.axis_index("tm") * t_rows
    ahead = passed_along(bold[:MAXD], "tm", -1)
    extended = jnp.concatenate([bold, ahead], 0)
    runs_pad = jnp.concatenate([runs, jnp.full((MAXD,), -1, jnp.int32)])
    own_runs = lax.dynamic_slice_in_dim(runs, first, t_rows)
    positions = first + jnp.arange(t_rows, dtype=jnp.int32)
    lagged_list = []
    for slot in range(DELAYS):
        offset = delays[slot]
        target_runs = lax.dynamic_slice_in_dim(runs_pad, first + offset, t_rows)
        valid = (positions + offset < total_rows) & (target_runs == own_runs)
        moved = lax.dynamic_slice_in_dim(extended, offset, t_rows, 0)
        lagged_list.append(jnp.where(valid[:, None], moved, jnp.zeros_like(moved)))
    stacked = jnp.stack(lagged_list, 1).reshape(t_rows, DELAYS * v_cols)
    cross = contract_rows(hidden, stacked)
    partial_cov = cross.reshape(d_local * DELAYS, v_cols).astype(jnp.bfloat16)
    panel_rows = lax.all_gather(panel, "tm", axis=0, tiled=True)
    rotated_part = contract_rows(
        lax.all_gather(panel_rows, "voxel", axis=1, tiled=True), partial_cov
    )
    rotated = lax.psum(rotated_part.astype(jnp.bfloat16), ("feature", "tm")).astype(jnp.float32)
    return scaled_by(rotated, eigvals, ridge_grid, total_rows)


def swapped(value, voxel, feature, tm):
    sizes = (lax.axis_size("voxel"), lax.axis_size("feature"), lax.axis_size("tm"))
    pairs = []
    for v in range(sizes[0]):
        for f in range(sizes[1]):
            for t in range(sizes[2]):
                source = (v * sizes[1] + f) * sizes[2] + t
                target = ((v ^ voxel) * sizes[1] + (f ^ feature)) * sizes[2] + (t ^ tm)
                pairs.append((source, target))
    return lax.ppermute(value, ("voxel", "feature", "tm"), pairs)


GROUPS = 4


def sort_matrices(sort):
    width = LANES // GROUPS
    row = lax.broadcasted_iota(jnp.int32, (sort.shape[1], LANES), 0)
    lane = lax.broadcasted_iota(jnp.int32, (sort.shape[1], LANES), 1)
    gap = row - DELAYS * (lane % width)
    for n in range(GROUPS):
        slot = (lane // width - n) % GROUPS
        for t in range(DELAYS // GROUPS):
            sort[n, :, t * LANES:(t + 1) * LANES] = (gap - slot == GROUPS * t).astype(F32).astype(BF16)


def sort_into(ordered, panel_t, sort):
    rows = panel_t.shape[0]
    block = sort.shape[1]
    width = LANES // GROUPS
    tiles = panel_t.shape[1] // (GROUPS * block)
    mixed = [
        jnp.dot(
            jnp.concatenate(
                [panel_t[:, (GROUPS * m + n) * block:(GROUPS * m + n + 1) * block] for m in range(tiles)], 0
            ),
            sort[n], preferred_element_type=F32,
        )
        for n in range(GROUPS)
    ]
    lane = lax.broadcasted_iota(jnp.int32, (rows, LANES), 1)
    for m in range(tiles):
        for t in range(DELAYS // GROUPS):
            parts = [part[m * rows:(m + 1) * rows, t * LANES:(t + 1) * LANES] for part in mixed]
            for r in range(GROUPS):
                tile = parts[(GROUPS - 1 - r) % GROUPS]
                for place in range(GROUPS - 2, -1, -1):
                    tile = jnp.where(lane < (place + 1) * width, parts[(place - r) % GROUPS], tile)
                if r:
                    tile = pltpu.roll(tile, LANES - r * width, 1)
                k = t * GROUPS + r
                ordered[k * rows:(k + 1) * rows, m * LANES:(m + 1) * LANES] = tile.astype(BF16)


def lag_sums(products, valid, shift, total):
    p_cols = total.shape[0]
    tiles = products.shape[1] // LANES
    places = valid.shape[0] // DELAYS
    stacked = []
    for j in range(tiles):
        parts = []
        for k in range(DELAYS):
            mask = valid[k * places + j:k * places + j + 1, :]
            part = products[k * p_cols:(k + 1) * p_cols, j * LANES:(j + 1) * LANES]
            parts.append((part * mask).astype(BF16))
        stacked.append(jnp.concatenate(parts, 1))
    moved = jnp.dot(jnp.concatenate(stacked, 0), shift[...], preferred_element_type=F32)
    for j in range(tiles + 1):
        at = slice(j * LANES, (j + 1) * LANES)
        add = total[:, at]
        if j < tiles:
            add = add + moved[j * p_cols:(j + 1) * p_cols, :LANES]
        if j > 0:
            add = add + moved[(j - 1) * p_cols:j * p_cols, LANES:]
        total[:, at] = add


def product(ordered, hidden):
    return lax.dot_general(
        ordered[...], hidden[...], (((1,), (1,)), ((), ())), preferred_element_type=F32
    )


def feature_copy(hidden, block, target, sem):
    width = target.shape[1]
    return pltpu.make_async_copy(
        hidden.at[:, pl.ds(pl.multiple_of(block * width, width), width)], target, sem
    )


def early_kernel(
    delays_in, panel_t, panel_core, hidden, runs, total, sort, valid, shift,
    delays, here, all_valid, products, ordered, loaded, hidden_own, hidden_core, sems,
):
    rows = hidden.shape[0]
    tiles, kept = rows // LANES, valid.shape[0] // DELAYS
    tm = lax.axis_index("tm")
    copies = [
        pltpu.make_async_copy(delays_in, delays, sems.at[0]),
        pltpu.make_async_copy(runs, here, sems.at[1]),
        pltpu.make_async_copy(panel_t, loaded, sems.at[2]),
        feature_copy(hidden, tm, hidden_own, sems.at[3]),
        feature_copy(hidden, tm ^ 1, hidden_core, sems.at[4]),
    ]
    for copy in copies:
        copy.start()
    sort_matrices(sort)
    total[...] = jnp.zeros_like(total)
    copies[2].wait()
    sort_into(ordered, loaded[...], sort)
    copies[3].wait()
    products[...] = product(ordered, hidden_own)
    sort_into(ordered, panel_core[...], sort)
    copies[0].wait()
    copies[1].wait()
    places = here.shape[0]
    now = here[...]
    place = lax.broadcasted_iota(jnp.int32, now.shape, 0)
    lane = lax.broadcasted_iota(jnp.int32, now.shape, 1)
    later = jnp.where(place == places - 1, -1, pltpu.roll(now, places - 1, 0))
    row = lax.broadcasted_iota(jnp.int32, (LANES, 2 * LANES), 0)
    col = lax.broadcasted_iota(jnp.int32, (LANES, 2 * LANES), 1)
    for k in range(DELAYS):
        back = LANES - delays[k]
        target = jnp.where(lane < back, pltpu.roll(now, back, 1), pltpu.roll(later, back, 1))
        all_valid[k * places:(k + 1) * places, :] = (target == now).astype(F32)
        valid[k * kept:k * kept + tiles, :] = all_valid[pl.ds(k * places + tm * tiles, tiles), :]
        shift[k * LANES:(k + 1) * LANES, :] = (col - row == delays[k]).astype(F32).astype(BF16)
    copies[4].wait()
    products[...] += product(ordered, hidden_core)
    lag_sums(products, valid, shift, total)


def add_part(panel_t, sort, hidden, valid, shift, total, ordered, products):
    sort_into(ordered, panel_t[...], sort)
    products[...] = product(ordered, hidden)
    lag_sums(products, valid, shift, total)


def own_kernel(panel_t, sort, hidden, valid, shift, earlier, total, ordered, products):
    total[...] = earlier[...]
    add_part(panel_t, sort, hidden, valid, shift, total, ordered, products)


def late_kernel(
    panel_t, sort, hidden, valid, shift, earlier, bold, bold_x, ahead, out, ordered, products, total,
):
    rows, v_cols = bold.shape
    total[...] = earlier[...]
    add_part(panel_t, sort, hidden, valid, shift, total, ordered, products)
    mine = total[:, :rows].astype(BF16)
    beyond = total[:, rows:].astype(BF16)
    blank = jnp.zeros((LANES - ahead.shape[0], v_cols), BF16)
    for place, part in enumerate((bold, bold_x)):
        cols = slice(place * v_cols, (place + 1) * v_cols)
        out[:, cols] = jnp.dot(mine, part[...], preferred_element_type=F32) + jnp.dot(
            beyond, jnp.concatenate([ahead[:, cols], blank], 0), preferred_element_type=F32
        )


def head_kernel(bold, bold_x, head):
    v_cols = bold.shape[1]
    for place, part in enumerate((bold, bold_x)):
        head[:, place * v_cols:(place + 1) * v_cols] = part[:16, :]


PARTS = 8


def scale_kernel(rotated, scale, out, scaled, sems):
    step = scaled.shape[0] // PARTS
    total = rotated[...]
    copies = []
    for part in range(PARTS):
        for r in range(part * step, (part + 1) * step):
            scaled[r] = (total * scale[r]).astype(BF16)
        rows = pl.ds(part * step, step)
        copies.append(pltpu.make_async_copy(scaled.at[rows], out.at[rows], sems.at[part]))
        copies[-1].start()
    for copy in copies:
        copy.wait()


def call(kernel, operands, out_shape, scratch, outside=()):
    hbm = pl.BlockSpec(memory_space=pltpu.HBM)
    operands = [
        pltpu.with_memory_space_constraint(operand, pltpu.HBM) if n in outside else operand
        for n, operand in enumerate(operands)
    ]
    vmem = pl.BlockSpec(memory_space=pltpu.VMEM)
    return pl.pallas_call(
        kernel,
        out_shape=out_shape,
        in_specs=[
            hbm if n in outside else vmem
            for n, operand in enumerate(operands)
        ],
        out_specs=jax.tree.map(lambda _: vmem, out_shape),
        scratch_shapes=scratch,
        compiler_params=pltpu.CompilerParams(vmem_limit_bytes=12 * 1024 * 1024),
        cost_estimate=pl.CostEstimate(flops=1024, bytes_accessed=1024, transcendentals=0),
    )(*operands)


def after(value, done):
    return lax.optimization_barrier((value, done))[0]


def exchanged(hidden, bold, panel, eigvals, ridge_grid, delays, runs):
    t_rows, d_local = hidden.shape
    v_cols = bold.shape[1]
    p_cols = panel.shape[1]
    tm_count = lax.axis_size("tm")
    total_rows = t_rows * tm_count
    width = d_local // tm_count
    block = DELAYS * LANES
    tm = lax.axis_index("tm")
    voxel = lax.axis_index("voxel")
    reach = t_rows + LANES
    dma = pltpu.SemaphoreType.DMA

    panel_t = panel.T
    late_t = swapped(panel_t, 0, 0, 2)
    panel_core = swapped(panel_t, 0, 0, 1)
    bold_x = swapped(bold, 1, 0, 0)

    places = runs.shape[0] // LANES
    features = pltpu.VMEM((t_rows, width), BF16)
    ordered = pltpu.VMEM((DELAYS * p_cols, width), BF16)
    products = pltpu.VMEM((DELAYS * p_cols, t_rows), F32)
    total = jax.ShapeDtypeStruct((p_cols, reach), F32)
    earlier, sort, valid, shift = call(
        early_kernel, (delays, panel_t, panel_core, hidden, runs.reshape(places, LANES)),
        (total, jax.ShapeDtypeStruct((GROUPS, block // GROUPS, block // GROUPS), BF16),
         jax.ShapeDtypeStruct((DELAYS * -(-t_rows // (8 * LANES)) * 8, LANES), F32), jax.ShapeDtypeStruct((block, 2 * LANES), BF16)),
        [pltpu.SMEM(delays.shape, jnp.int32), pltpu.VMEM((places, LANES), jnp.int32),
         pltpu.VMEM((DELAYS * places, LANES), F32),
         products, ordered, pltpu.VMEM(panel_t.shape, BF16), features, features, dma((5,))], (0, 1, 3, 4),
    )
    penalty = 2.0 ** ((ridge_grid.astype(F32) - 8.0) * 0.5)
    scale = 1.0 / (math.sqrt(total_rows) * (eigvals[None, :] + penalty[:, None]))
    scale = jnp.broadcast_to(scale[:, :, None], (*scale.shape, v_cols))
    head = call(
        head_kernel, (bold, after(bold_x, (earlier, scale))), jax.ShapeDtypeStruct((16, 2 * v_cols), BF16), []
    )
    ahead = passed_along(head, "tm", -1)
    hidden_late = after(hidden, head)
    hidden_own = lax.dynamic_slice_in_dim(hidden_late, (tm ^ 2) * width, width, 1)
    hidden_core = lax.dynamic_slice_in_dim(hidden_late, (tm ^ 3) * width, width, 1)
    late_t = after(late_t, (ahead, hidden_own, hidden_core))
    late_core = swapped(late_t, 0, 0, 1)
    earlier = call(
        own_kernel, (late_t, sort, hidden_own, valid, shift, earlier), total, [ordered, products]
    )
    part = call(
        late_kernel,
        (after(late_core, earlier), sort, hidden_core, valid, shift, earlier, bold, bold_x, ahead),
        jax.ShapeDtypeStruct((p_cols, 2 * v_cols), F32),
        [ordered, products, pltpu.VMEM((p_cols, reach), F32)],
    )

    part = part.astype(BF16)
    part = part.astype(F32) + swapped(part, 0, 0, 1).astype(F32)
    mine, theirs = part[:, :v_cols].astype(BF16), part[:, v_cols:].astype(BF16)
    from_x = swapped(theirs, 1, 0, 1)
    from_xy = swapped(theirs, 1, 0, 3)
    from_y = swapped(mine, 0, 0, 3)
    from_y, from_x, from_xy = lax.optimization_barrier((from_y, from_x, from_xy))
    near = mine.astype(F32) + from_y.astype(F32)
    far = from_x.astype(F32) + from_xy.astype(F32)
    rotated = jnp.where(
        voxel == 0, jnp.concatenate([near, far], 0), jnp.concatenate([far, near], 0)
    )
    for step in (1, 2):
        rounded = rotated.astype(BF16)
        rotated = rounded.astype(F32) + swapped(rounded, 0, step, 1).astype(F32)
    shape = (ridge_grid.shape[0], 2 * p_cols, v_cols)
    return pl.pallas_call(
        scale_kernel,
        out_shape=jax.ShapeDtypeStruct(shape, BF16),
        in_specs=2 * [pl.BlockSpec(memory_space=pltpu.VMEM)],
        out_specs=pl.BlockSpec(memory_space=pl.ANY),
        scratch_shapes=[pltpu.VMEM(shape, BF16), dma((PARTS,))],
        compiler_params=pltpu.CompilerParams(vmem_limit_bytes=4 * 1024 * 1024),
    )(rotated, scale)


def solution(mesh):
    sizes = (mesh.shape["voxel"], mesh.shape["feature"], mesh.shape["tm"])
    shards = exchanged if sizes == (2, 4, 4) else gathered
    return jax.shard_map(
        shards,
        mesh=mesh,
        in_specs=(
            P("tm", "feature"),
            P("tm", "voxel"),
            P(("feature", "tm"), "voxel"),
            P(),
            P(),
            P(),
            P(),
        ),
        out_specs=P(None, None, "voxel"),
        check_vma=False,
    )
```

```python
import math

import jax
import jax.numpy as jnp
from jax import lax
from jax.experimental import pallas as pl
from jax.experimental.pallas import tpu as pltpu
from jax.sharding import PartitionSpec as P

DELAYS = 8
MAXD = 12
LANES = 128
F32 = jnp.float32
BF16 = jnp.bfloat16


def passed_along(value, axis, steps):
    count = lax.axis_size(axis)
    first, last = (max(0, -steps), min(count, count - steps))
    return lax.ppermute(value, axis, [(source, source + steps) for source in range(first, last)])


def contract_rows(left, right):
    return lax.dot_general(
        left, right, (((0,), (0,)), ((), ())), preferred_element_type=jnp.float32
    )


def scaled_by(rotated, eigvals, ridge_grid, total_rows):
    penalty = 2.0 ** ((ridge_grid.astype(jnp.float32) - 8.0) * 0.5)
    scaled = rotated[None] / (
        math.sqrt(total_rows) * (eigvals[None, :, None] + penalty[:, None, None])
    )
    return scaled.astype(jnp.bfloat16)


def gathered(hidden, bold, panel, eigvals, ridge_grid, delays, runs):
    t_rows = hidden.shape[0]
    d_local = hidden.shape[1]
    v_cols = bold.shape[1]
    total_rows = t_rows * lax.axis_size("tm")
    first = lax.axis_index("tm") * t_rows
    ahead = passed_along(bold[:MAXD], "tm", -1)
    extended = jnp.concatenate([bold, ahead], 0)
    runs_pad = jnp.concatenate([runs, jnp.full((MAXD,), -1, jnp.int32)])
    own_runs = lax.dynamic_slice_in_dim(runs, first, t_rows)
    positions = first + jnp.arange(t_rows, dtype=jnp.int32)
    lagged_list = []
    for slot in range(DELAYS):
        offset = delays[slot]
        target_runs = lax.dynamic_slice_in_dim(runs_pad, first + offset, t_rows)
        valid = (positions + offset < total_rows) & (target_runs == own_runs)
        moved = lax.dynamic_slice_in_dim(extended, offset, t_rows, 0)
        lagged_list.append(jnp.where(valid[:, None], moved, jnp.zeros_like(moved)))
    stacked = jnp.stack(lagged_list, 1).reshape(t_rows, DELAYS * v_cols)
    cross = contract_rows(hidden, stacked)
    partial_cov = cross.reshape(d_local * DELAYS, v_cols).astype(jnp.bfloat16)
    panel_rows = lax.all_gather(panel, "tm", axis=0, tiled=True)
    rotated_part = contract_rows(
        lax.all_gather(panel_rows, "voxel", axis=1, tiled=True), partial_cov
    )
    rotated = lax.psum(rotated_part.astype(jnp.bfloat16), ("feature", "tm")).astype(jnp.float32)
    return scaled_by(rotated, eigvals, ridge_grid, total_rows)


def swapped(value, voxel, feature, tm):
    sizes = (lax.axis_size("voxel"), lax.axis_size("feature"), lax.axis_size("tm"))
    pairs = []
    for v in range(sizes[0]):
        for f in range(sizes[1]):
            for t in range(sizes[2]):
                source = (v * sizes[1] + f) * sizes[2] + t
                target = ((v ^ voxel) * sizes[1] + (f ^ feature)) * sizes[2] + (t ^ tm)
                pairs.append((source, target))
    return lax.ppermute(value, ("voxel", "feature", "tm"), pairs)


GROUPS = 4


def sort_matrices(sort):
    width = LANES // GROUPS
    row = lax.broadcasted_iota(jnp.int32, (sort.shape[1], LANES), 0)
    lane = lax.broadcasted_iota(jnp.int32, (sort.shape[1], LANES), 1)
    gap = row - DELAYS * (lane % width)
    for n in range(GROUPS):
        slot = (lane // width - n) % GROUPS
        for t in range(DELAYS // GROUPS):
            sort[n, :, t * LANES:(t + 1) * LANES] = (gap - slot == GROUPS * t).astype(F32).astype(BF16)


def sort_into(ordered, panel_t, sort):
    rows = panel_t.shape[0]
    block = sort.shape[1]
    width = LANES // GROUPS
    tiles = panel_t.shape[1] // (GROUPS * block)
    mixed = [
        jnp.dot(
            jnp.concatenate(
                [panel_t[:, (GROUPS * m + n) * block:(GROUPS * m + n + 1) * block] for m in range(tiles)], 0
            ),
            sort[n], preferred_element_type=F32,
        )
        for n in range(GROUPS)
    ]
    lane = lax.broadcasted_iota(jnp.int32, (rows, LANES), 1)
    for m in range(tiles):
        for t in range(DELAYS // GROUPS):
            parts = [part[m * rows:(m + 1) * rows, t * LANES:(t + 1) * LANES] for part in mixed]
            for r in range(GROUPS):
                tile = parts[(GROUPS - 1 - r) % GROUPS]
                for place in range(GROUPS - 2, -1, -1):
                    tile = jnp.where(lane < (place + 1) * width, parts[(place - r) % GROUPS], tile)
                if r:
                    tile = pltpu.roll(tile, LANES - r * width, 1)
                k = t * GROUPS + r
                ordered[k * rows:(k + 1) * rows, m * LANES:(m + 1) * LANES] = tile.astype(BF16)


def lag_sums(products, valid, shift, total):
    p_cols = total.shape[0]
    tiles = products.shape[1] // LANES
    places = valid.shape[0] // DELAYS
    stacked = []
    for j in range(tiles):
        parts = []
        for k in range(DELAYS):
            mask = valid[k * places + j:k * places + j + 1, :]
            part = products[k * p_cols:(k + 1) * p_cols, j * LANES:(j + 1) * LANES]
            parts.append((part * mask).astype(BF16))
        stacked.append(jnp.concatenate(parts, 1))
    moved = jnp.dot(jnp.concatenate(stacked, 0), shift[...], preferred_element_type=F32)
    for j in range(tiles + 1):
        at = slice(j * LANES, (j + 1) * LANES)
        add = total[:, at]
        if j < tiles:
            add = add + moved[j * p_cols:(j + 1) * p_cols, :LANES]
        if j > 0:
            add = add + moved[(j - 1) * p_cols:j * p_cols, LANES:]
        total[:, at] = add


def product(ordered, hidden):
    return lax.dot_general(
        ordered[...], hidden[...], (((1,), (1,)), ((), ())), preferred_element_type=F32
    )


def feature_copy(hidden, block, target, sem):
    width = target.shape[1]
    return pltpu.make_async_copy(
        hidden.at[:, pl.ds(pl.multiple_of(block * width, width), width)], target, sem
    )


def early_kernel(
    delays_in, panel_t, panel_core, hidden, runs, total, sort, valid, shift,
    delays, here, all_valid, products, ordered, loaded, hidden_own, hidden_core, sems,
):
    rows = hidden.shape[0]
    tiles, kept = rows // LANES, valid.shape[0] // DELAYS
    tm = lax.axis_index("tm")
    copies = [
        pltpu.make_async_copy(delays_in, delays, sems.at[0]),
        pltpu.make_async_copy(runs, here, sems.at[1]),
        pltpu.make_async_copy(panel_t, loaded, sems.at[2]),
        feature_copy(hidden, tm, hidden_own, sems.at[3]),
        feature_copy(hidden, tm ^ 1, hidden_core, sems.at[4]),
    ]
    for copy in copies:
        copy.start()
    sort_matrices(sort)
    total[...] = jnp.zeros_like(total)
    copies[2].wait()
    sort_into(ordered, loaded[...], sort)
    copies[3].wait()
    products[...] = product(ordered, hidden_own)
    sort_into(ordered, panel_core[...], sort)
    copies[0].wait()
    copies[1].wait()
    places = here.shape[0]
    now = here[...]
    place = lax.broadcasted_iota(jnp.int32, now.shape, 0)
    lane = lax.broadcasted_iota(jnp.int32, now.shape, 1)
    later = jnp.where(place == places - 1, -1, pltpu.roll(now, places - 1, 0))
    row = lax.broadcasted_iota(jnp.int32, (LANES, 2 * LANES), 0)
    col = lax.broadcasted_iota(jnp.int32, (LANES, 2 * LANES), 1)
    for k in range(DELAYS):
        back = LANES - delays[k]
        target = jnp.where(lane < back, pltpu.roll(now, back, 1), pltpu.roll(later, back, 1))
        all_valid[k * places:(k + 1) * places, :] = (target == now).astype(F32)
        valid[k * kept:k * kept + tiles, :] = all_valid[pl.ds(k * places + tm * tiles, tiles), :]
        shift[k * LANES:(k + 1) * LANES, :] = (col - row == delays[k]).astype(F32).astype(BF16)
    copies[4].wait()
    products[...] += product(ordered, hidden_core)
    lag_sums(products, valid, shift, total)


def add_part(panel_t, sort, hidden, valid, shift, total, ordered, products):
    sort_into(ordered, panel_t[...], sort)
    products[...] = product(ordered, hidden)
    lag_sums(products, valid, shift, total)


def own_kernel(panel_t, sort, hidden, valid, shift, earlier, total, ordered, products):
    total[...] = earlier[...]
    add_part(panel_t, sort, hidden, valid, shift, total, ordered, products)


def late_kernel(
    panel_t, sort, hidden, valid, shift, earlier, bold, bold_x, ahead, out, ordered, products, total,
):
    rows, v_cols = bold.shape
    total[...] = earlier[...]
    add_part(panel_t, sort, hidden, valid, shift, total, ordered, products)
    mine = total[:, :rows].astype(BF16)
    beyond = total[:, rows:].astype(BF16)
    blank = jnp.zeros((LANES - ahead.shape[0], v_cols), BF16)
    for place, part in enumerate((bold, bold_x)):
        cols = slice(place * v_cols, (place + 1) * v_cols)
        out[:, cols] = jnp.dot(mine, part[...], preferred_element_type=F32) + jnp.dot(
            beyond, jnp.concatenate([ahead[:, cols], blank], 0), preferred_element_type=F32
        )


def head_kernel(bold, bold_x, head):
    v_cols = bold.shape[1]
    for place, part in enumerate((bold, bold_x)):
        head[:, place * v_cols:(place + 1) * v_cols] = part[:16, :]


PARTS = 8


def scale_kernel(rotated, scale, out, scaled, sems):
    step = scaled.shape[0] // PARTS
    total = rotated[...]
    copies = []
    for part in range(PARTS):
        for r in range(part * step, (part + 1) * step):
            scaled[r] = (total * scale[r]).astype(BF16)
        rows = pl.ds(part * step, step)
        copies.append(pltpu.make_async_copy(scaled.at[rows], out.at[rows], sems.at[part]))
        copies[-1].start()
    for copy in copies:
        copy.wait()


def call(kernel, operands, out_shape, scratch, outside=()):
    hbm = pl.BlockSpec(memory_space=pltpu.HBM)
    operands = [
        pltpu.with_memory_space_constraint(operand, pltpu.HBM) if n in outside else operand
        for n, operand in enumerate(operands)
    ]
    vmem = pl.BlockSpec(memory_space=pltpu.VMEM)
    return pl.pallas_call(
        kernel,
        out_shape=out_shape,
        in_specs=[
            hbm if n in outside else vmem
            for n, operand in enumerate(operands)
        ],
        out_specs=jax.tree.map(lambda _: vmem, out_shape),
        scratch_shapes=scratch,
        compiler_params=pltpu.CompilerParams(vmem_limit_bytes=12 * 1024 * 1024),
        cost_estimate=pl.CostEstimate(flops=1024, bytes_accessed=1024, transcendentals=0),
    )(*operands)


def after(value, done):
    return lax.optimization_barrier((value, done))[0]


def exchanged(hidden, bold, panel, eigvals, ridge_grid, delays, runs):
    t_rows, d_local = hidden.shape
    v_cols = bold.shape[1]
    p_cols = panel.shape[1]
    tm_count = lax.axis_size("tm")
    total_rows = t_rows * tm_count
    width = d_local // tm_count
    block = DELAYS * LANES
    tm = lax.axis_index("tm")
    voxel = lax.axis_index("voxel")
    reach = t_rows + LANES
    dma = pltpu.SemaphoreType.DMA

    panel_t = panel.T
    late_t = swapped(panel_t, 0, 0, 3)
    panel_core = swapped(panel_t, 0, 0, 1)
    bold_x = swapped(bold, 1, 0, 0)

    places = runs.shape[0] // LANES
    features = pltpu.VMEM((t_rows, width), BF16)
    ordered = pltpu.VMEM((DELAYS * p_cols, width), BF16)
    products = pltpu.VMEM((DELAYS * p_cols, t_rows), F32)
    total = jax.ShapeDtypeStruct((p_cols, reach), F32)
    earlier, sort, valid, shift = call(
        early_kernel, (delays, panel_t, panel_core, hidden, runs.reshape(places, LANES)),
        (total, jax.ShapeDtypeStruct((GROUPS, block // GROUPS, block // GROUPS), BF16),
         jax.ShapeDtypeStruct((DELAYS * -(-t_rows // (8 * LANES)) * 8, LANES), F32), jax.ShapeDtypeStruct((block, 2 * LANES), BF16)),
        [pltpu.SMEM(delays.shape, jnp.int32), pltpu.VMEM((places, LANES), jnp.int32),
         pltpu.VMEM((DELAYS * places, LANES), F32),
         products, ordered, pltpu.VMEM(panel_t.shape, BF16), features, features, dma((5,))], (0, 1, 3, 4),
    )
    penalty = 2.0 ** ((ridge_grid.astype(F32) - 8.0) * 0.5)
    scale = 1.0 / (math.sqrt(total_rows) * (eigvals[None, :] + penalty[:, None]))
    scale = jnp.broadcast_to(scale[:, :, None], (*scale.shape, v_cols))
    head = call(
        head_kernel, (bold, after(bold_x, (earlier, scale))), jax.ShapeDtypeStruct((16, 2 * v_cols), BF16), []
    )
    ahead = passed_along(head, "tm", -1)
    hidden_late = after(hidden, head)
    hidden_own = lax.dynamic_slice_in_dim(hidden_late, (tm ^ 3) * width, width, 1)
    hidden_core = lax.dynamic_slice_in_dim(hidden_late, (tm ^ 2) * width, width, 1)
    late_t = after(late_t, (ahead, hidden_own, hidden_core))
    late_core = swapped(late_t, 0, 0, 1)
    earlier = call(
        own_kernel, (late_t, sort, hidden_own, valid, shift, earlier), total, [ordered, products]
    )
    part = call(
        late_kernel,
        (after(late_core, earlier), sort, hidden_core, valid, shift, earlier, bold, bold_x, ahead),
        jax.ShapeDtypeStruct((p_cols, 2 * v_cols), F32),
        [ordered, products, pltpu.VMEM((p_cols, reach), F32)],
    )

    part = part.astype(BF16)
    part = part.astype(F32) + swapped(part, 0, 0, 1).astype(F32)
    mine, theirs = part[:, :v_cols].astype(BF16), part[:, v_cols:].astype(BF16)
    from_x = swapped(theirs, 1, 0, 1)
    from_xy = swapped(theirs, 1, 0, 3)
    from_y = swapped(mine, 0, 0, 3)
    from_y, from_x, from_xy = lax.optimization_barrier((from_y, from_x, from_xy))
    near = mine.astype(F32) + from_y.astype(F32)
    far = from_x.astype(F32) + from_xy.astype(F32)
    rotated = jnp.where(
        voxel == 0, jnp.concatenate([near, far], 0), jnp.concatenate([far, near], 0)
    )
    for step in (1, 2):
        rounded = rotated.astype(BF16)
        rotated = rounded.astype(F32) + swapped(rounded, 0, step, 1).astype(F32)
    shape = (ridge_grid.shape[0], 2 * p_cols, v_cols)
    return pl.pallas_call(
        scale_kernel,
        out_shape=jax.ShapeDtypeStruct(shape, BF16),
        in_specs=2 * [pl.BlockSpec(memory_space=pltpu.VMEM)],
        out_specs=pl.BlockSpec(memory_space=pl.ANY),
        scratch_shapes=[pltpu.VMEM(shape, BF16), dma((PARTS,))],
        compiler_params=pltpu.CompilerParams(vmem_limit_bytes=4 * 1024 * 1024),
    )(rotated, scale)


def solution(mesh):
    sizes = (mesh.shape["voxel"], mesh.shape["feature"], mesh.shape["tm"])
    shards = exchanged if sizes == (2, 4, 4) else gathered
    return jax.shard_map(
        shards,
        mesh=mesh,
        in_specs=(
            P("tm", "feature"),
            P("tm", "voxel"),
            P(("feature", "tm"), "voxel"),
            P(),
            P(),
            P(),
            P(),
        ),
        out_specs=P(None, None, "voxel"),
        check_vma=False,
    )
```

```python
import math

import jax
import jax.numpy as jnp
from jax import lax
from jax.experimental import pallas as pl
from jax.experimental.pallas import tpu as pltpu
from jax.sharding import PartitionSpec as P

DELAYS = 8
MAXD = 12
LANES = 128
F32 = jnp.float32
BF16 = jnp.bfloat16


def passed_along(value, axis, steps):
    count = lax.axis_size(axis)
    first, last = (max(0, -steps), min(count, count - steps))
    return lax.ppermute(value, axis, [(source, source + steps) for source in range(first, last)])


def contract_rows(left, right):
    return lax.dot_general(
        left, right, (((0,), (0,)), ((), ())), preferred_element_type=jnp.float32
    )


def scaled_by(rotated, eigvals, ridge_grid, total_rows):
    penalty = 2.0 ** ((ridge_grid.astype(jnp.float32) - 8.0) * 0.5)
    scaled = rotated[None] / (
        math.sqrt(total_rows) * (eigvals[None, :, None] + penalty[:, None, None])
    )
    return scaled.astype(jnp.bfloat16)


def gathered(hidden, bold, panel, eigvals, ridge_grid, delays, runs):
    t_rows = hidden.shape[0]
    d_local = hidden.shape[1]
    v_cols = bold.shape[1]
    total_rows = t_rows * lax.axis_size("tm")
    first = lax.axis_index("tm") * t_rows
    ahead = passed_along(bold[:MAXD], "tm", -1)
    extended = jnp.concatenate([bold, ahead], 0)
    runs_pad = jnp.concatenate([runs, jnp.full((MAXD,), -1, jnp.int32)])
    own_runs = lax.dynamic_slice_in_dim(runs, first, t_rows)
    positions = first + jnp.arange(t_rows, dtype=jnp.int32)
    lagged_list = []
    for slot in range(DELAYS):
        offset = delays[slot]
        target_runs = lax.dynamic_slice_in_dim(runs_pad, first + offset, t_rows)
        valid = (positions + offset < total_rows) & (target_runs == own_runs)
        moved = lax.dynamic_slice_in_dim(extended, offset, t_rows, 0)
        lagged_list.append(jnp.where(valid[:, None], moved, jnp.zeros_like(moved)))
    stacked = jnp.stack(lagged_list, 1).reshape(t_rows, DELAYS * v_cols)
    cross = contract_rows(hidden, stacked)
    partial_cov = cross.reshape(d_local * DELAYS, v_cols).astype(jnp.bfloat16)
    panel_rows = lax.all_gather(panel, "tm", axis=0, tiled=True)
    rotated_part = contract_rows(
        lax.all_gather(panel_rows, "voxel", axis=1, tiled=True), partial_cov
    )
    rotated = lax.psum(rotated_part.astype(jnp.bfloat16), ("feature", "tm")).astype(jnp.float32)
    return scaled_by(rotated, eigvals, ridge_grid, total_rows)


def swapped(value, voxel, feature, tm):
    sizes = (lax.axis_size("voxel"), lax.axis_size("feature"), lax.axis_size("tm"))
    pairs = []
    for v in range(sizes[0]):
        for f in range(sizes[1]):
            for t in range(sizes[2]):
                source = (v * sizes[1] + f) * sizes[2] + t
                target = ((v ^ voxel) * sizes[1] + (f ^ feature)) * sizes[2] + (t ^ tm)
                pairs.append((source, target))
    return lax.ppermute(value, ("voxel", "feature", "tm"), pairs)


GROUPS = 4


def as_sent(value):
    return lax.reduce_precision(value, 8, 7)


def received(value, voxel, feature, tm):
    return swapped(value.astype(BF16), voxel, feature, tm).astype(F32)


def sort_matrices(sort):
    width = LANES // GROUPS
    row = lax.broadcasted_iota(jnp.int32, (sort.shape[1], LANES), 0)
    lane = lax.broadcasted_iota(jnp.int32, (sort.shape[1], LANES), 1)
    gap = row - DELAYS * (lane % width)
    for n in range(GROUPS):
        slot = (lane // width - n) % GROUPS
        for t in range(DELAYS // GROUPS):
            sort[n, :, t * LANES:(t + 1) * LANES] = (gap - slot == GROUPS * t).astype(F32).astype(BF16)


def sort_into(ordered, panel_t, sort):
    rows = panel_t.shape[0]
    block = sort.shape[1]
    width = LANES // GROUPS
    tiles = panel_t.shape[1] // (GROUPS * block)
    mixed = [
        jnp.dot(
            jnp.concatenate(
                [panel_t[:, (GROUPS * m + n) * block:(GROUPS * m + n + 1) * block] for m in range(tiles)], 0
            ),
            sort[n], preferred_element_type=F32,
        )
        for n in range(GROUPS)
    ]
    lane = lax.broadcasted_iota(jnp.int32, (rows, LANES), 1)
    for m in range(tiles):
        for t in range(DELAYS // GROUPS):
            parts = [part[m * rows:(m + 1) * rows, t * LANES:(t + 1) * LANES] for part in mixed]
            for r in range(GROUPS):
                tile = parts[(GROUPS - 1 - r) % GROUPS]
                for place in range(GROUPS - 2, -1, -1):
                    tile = jnp.where(lane < (place + 1) * width, parts[(place - r) % GROUPS], tile)
                if r:
                    tile = pltpu.roll(tile, LANES - r * width, 1)
                k = t * GROUPS + r
                ordered[k * rows:(k + 1) * rows, m * LANES:(m + 1) * LANES] = tile.astype(BF16)


def lag_sums(products, valid, shift, total):
    p_cols = total.shape[0]
    tiles = products.shape[1] // LANES
    places = valid.shape[0] // DELAYS
    stacked = []
    for j in range(tiles):
        parts = []
        for k in range(DELAYS):
            mask = valid[k * places + j:k * places + j + 1, :]
            part = products[k * p_cols:(k + 1) * p_cols, j * LANES:(j + 1) * LANES]
            parts.append((part * mask).astype(BF16))
        stacked.append(jnp.concatenate(parts, 1))
    moved = jnp.dot(jnp.concatenate(stacked, 0), shift[...], preferred_element_type=F32)
    for j in range(tiles + 1):
        at = slice(j * LANES, (j + 1) * LANES)
        add = total[:, at]
        if j < tiles:
            add = add + moved[j * p_cols:(j + 1) * p_cols, :LANES]
        if j > 0:
            add = add + moved[(j - 1) * p_cols:j * p_cols, LANES:]
        total[:, at] = add


def product(ordered, hidden):
    return lax.dot_general(
        ordered[...], hidden[...], (((1,), (1,)), ((), ())), preferred_element_type=F32
    )


def feature_copy(hidden, block, target, sem):
    width = target.shape[1]
    return pltpu.make_async_copy(
        hidden.at[:, pl.ds(pl.multiple_of(block * width, width), width)], target, sem
    )


def early_kernel(
    delays_in, panel_t, panel_core, hidden, runs, total, sort, valid, shift,
    delays, here, all_valid, products, ordered, loaded, hidden_own, hidden_core, sems,
):
    rows = hidden.shape[0]
    tiles, kept = rows // LANES, valid.shape[0] // DELAYS
    tm = lax.axis_index("tm")
    copies = [
        pltpu.make_async_copy(delays_in, delays, sems.at[0]),
        pltpu.make_async_copy(runs, here, sems.at[1]),
        pltpu.make_async_copy(panel_t, loaded, sems.at[2]),
        feature_copy(hidden, tm, hidden_own, sems.at[3]),
        feature_copy(hidden, tm ^ 1, hidden_core, sems.at[4]),
    ]
    for copy in copies:
        copy.start()
    sort_matrices(sort)
    total[...] = jnp.zeros_like(total)
    copies[2].wait()
    sort_into(ordered, loaded[...], sort)
    copies[3].wait()
    products[...] = product(ordered, hidden_own)
    sort_into(ordered, panel_core[...], sort)
    copies[0].wait()
    copies[1].wait()
    places = here.shape[0]
    now = here[...]
    place = lax.broadcasted_iota(jnp.int32, now.shape, 0)
    lane = lax.broadcasted_iota(jnp.int32, now.shape, 1)
    later = jnp.where(place == places - 1, -1, pltpu.roll(now, places - 1, 0))
    row = lax.broadcasted_iota(jnp.int32, (LANES, 2 * LANES), 0)
    col = lax.broadcasted_iota(jnp.int32, (LANES, 2 * LANES), 1)
    for k in range(DELAYS):
        back = LANES - delays[k]
        target = jnp.where(lane < back, pltpu.roll(now, back, 1), pltpu.roll(later, back, 1))
        all_valid[k * places:(k + 1) * places, :] = (target == now).astype(F32)
        valid[k * kept:k * kept + tiles, :] = all_valid[pl.ds(k * places + tm * tiles, tiles), :]
        shift[k * LANES:(k + 1) * LANES, :] = (col - row == delays[k]).astype(F32).astype(BF16)
    copies[4].wait()
    products[...] += product(ordered, hidden_core)
    lag_sums(products, valid, shift, total)


def add_part(panel_t, sort, hidden, valid, shift, total, ordered, products):
    sort_into(ordered, panel_t[...], sort)
    products[...] = product(ordered, hidden)
    lag_sums(products, valid, shift, total)


def own_kernel(panel_t, sort, hidden, valid, shift, earlier, total, ordered, products):
    total[...] = earlier[...]
    add_part(panel_t, sort, hidden, valid, shift, total, ordered, products)


def late_kernel(
    panel_t, sort, hidden, valid, shift, earlier, bold, bold_x, ahead, out, ordered, products, total,
):
    rows, v_cols = bold.shape
    total[...] = earlier[...]
    add_part(panel_t, sort, hidden, valid, shift, total, ordered, products)
    mine = total[:, :rows].astype(BF16)
    beyond = total[:, rows:].astype(BF16)
    blank = jnp.zeros((LANES - ahead.shape[0], v_cols), BF16)
    for place, part in enumerate((bold, bold_x)):
        cols = slice(place * v_cols, (place + 1) * v_cols)
        out[:, cols] = jnp.dot(mine, part[...], preferred_element_type=F32) + jnp.dot(
            beyond, jnp.concatenate([ahead[:, cols], blank], 0), preferred_element_type=F32
        )


def head_kernel(bold, bold_x, head):
    v_cols = bold.shape[1]
    for place, part in enumerate((bold, bold_x)):
        head[:, place * v_cols:(place + 1) * v_cols] = part[:16, :]


PARTS = 8


def scale_kernel(rotated, scale, out, scaled, sems):
    step = scaled.shape[0] // PARTS
    total = rotated[...]
    copies = []
    for part in range(PARTS):
        for r in range(part * step, (part + 1) * step):
            scaled[r] = (total * scale[r]).astype(BF16)
        rows = pl.ds(part * step, step)
        copies.append(pltpu.make_async_copy(scaled.at[rows], out.at[rows], sems.at[part]))
        copies[-1].start()
    for copy in copies:
        copy.wait()


def call(kernel, operands, out_shape, scratch, outside=()):
    hbm = pl.BlockSpec(memory_space=pltpu.HBM)
    operands = [
        pltpu.with_memory_space_constraint(operand, pltpu.HBM) if n in outside else operand
        for n, operand in enumerate(operands)
    ]
    vmem = pl.BlockSpec(memory_space=pltpu.VMEM)
    return pl.pallas_call(
        kernel,
        out_shape=out_shape,
        in_specs=[
            hbm if n in outside else vmem
            for n, operand in enumerate(operands)
        ],
        out_specs=jax.tree.map(lambda _: vmem, out_shape),
        scratch_shapes=scratch,
        compiler_params=pltpu.CompilerParams(vmem_limit_bytes=12 * 1024 * 1024),
        cost_estimate=pl.CostEstimate(flops=1024, bytes_accessed=1024, transcendentals=0),
    )(*operands)


def after(value, done):
    return lax.optimization_barrier((value, done))[0]


def exchanged(hidden, bold, panel, eigvals, ridge_grid, delays, runs):
    t_rows, d_local = hidden.shape
    v_cols = bold.shape[1]
    p_cols = panel.shape[1]
    tm_count = lax.axis_size("tm")
    total_rows = t_rows * tm_count
    width = d_local // tm_count
    block = DELAYS * LANES
    tm = lax.axis_index("tm")
    voxel = lax.axis_index("voxel")
    reach = t_rows + LANES
    dma = pltpu.SemaphoreType.DMA

    panel_t = panel.T
    late_t = swapped(panel_t, 0, 0, 3)
    panel_core = swapped(panel_t, 0, 0, 1)
    bold_x = swapped(bold, 1, 0, 0)

    places = runs.shape[0] // LANES
    features = pltpu.VMEM((t_rows, width), BF16)
    ordered = pltpu.VMEM((DELAYS * p_cols, width), BF16)
    products = pltpu.VMEM((DELAYS * p_cols, t_rows), F32)
    total = jax.ShapeDtypeStruct((p_cols, reach), F32)
    earlier, sort, valid, shift = call(
        early_kernel, (delays, panel_t, panel_core, hidden, runs.reshape(places, LANES)),
        (total, jax.ShapeDtypeStruct((GROUPS, block // GROUPS, block // GROUPS), BF16),
         jax.ShapeDtypeStruct((DELAYS * -(-t_rows // (8 * LANES)) * 8, LANES), F32), jax.ShapeDtypeStruct((block, 2 * LANES), BF16)),
        [pltpu.SMEM(delays.shape, jnp.int32), pltpu.VMEM((places, LANES), jnp.int32),
         pltpu.VMEM((DELAYS * places, LANES), F32),
         products, ordered, pltpu.VMEM(panel_t.shape, BF16), features, features, dma((5,))], (0, 1, 3, 4),
    )
    penalty = 2.0 ** ((ridge_grid.astype(F32) - 8.0) * 0.5)
    scale = 1.0 / (math.sqrt(total_rows) * (eigvals[None, :] + penalty[:, None]))
    scale = jnp.broadcast_to(scale[:, :, None], (*scale.shape, v_cols))
    head = call(
        head_kernel, (bold, after(bold_x, (earlier, scale))), jax.ShapeDtypeStruct((16, 2 * v_cols), BF16), []
    )
    ahead = passed_along(head, "tm", -1)
    hidden_late = after(hidden, head)
    hidden_own = lax.dynamic_slice_in_dim(hidden_late, (tm ^ 3) * width, width, 1)
    hidden_core = lax.dynamic_slice_in_dim(hidden_late, (tm ^ 2) * width, width, 1)
    late_t = after(late_t, (ahead, hidden_own, hidden_core))
    late_core = swapped(late_t, 0, 0, 1)
    earlier = call(
        own_kernel, (late_t, sort, hidden_own, valid, shift, earlier), total, [ordered, products]
    )
    part = call(
        late_kernel,
        (after(late_core, earlier), sort, hidden_core, valid, shift, earlier, bold, bold_x, ahead),
        jax.ShapeDtypeStruct((p_cols, 2 * v_cols), F32),
        [ordered, products, pltpu.VMEM((p_cols, reach), F32)],
    )

    part = as_sent(part)
    part = as_sent(part + received(part, 0, 0, 1)).astype(BF16)
    mine, theirs = part[:, :v_cols], part[:, v_cols:]
    from_x = swapped(theirs.astype(BF16), 1, 0, 1)
    from_xy = swapped(theirs.astype(BF16), 1, 0, 3)
    from_y = swapped(mine.astype(BF16), 0, 0, 3)
    from_y, from_x, from_xy = lax.optimization_barrier((from_y, from_x, from_xy))
    near = mine.astype(F32) + from_y.astype(F32)
    far = from_x.astype(F32) + from_xy.astype(F32)
    rotated = jnp.where(
        voxel == 0, jnp.concatenate([near, far], 0), jnp.concatenate([far, near], 0)
    )
    for step in (1, 2):
        rotated = as_sent(rotated)
        rotated = rotated + received(rotated, 0, step, 1)
    shape = (ridge_grid.shape[0], 2 * p_cols, v_cols)
    return pl.pallas_call(
        scale_kernel,
        out_shape=jax.ShapeDtypeStruct(shape, BF16),
        in_specs=2 * [pl.BlockSpec(memory_space=pltpu.VMEM)],
        out_specs=pl.BlockSpec(memory_space=pl.ANY),
        scratch_shapes=[pltpu.VMEM(shape, BF16), dma((PARTS,))],
        compiler_params=pltpu.CompilerParams(vmem_limit_bytes=4 * 1024 * 1024),
    )(rotated, scale)


def solution(mesh):
    sizes = (mesh.shape["voxel"], mesh.shape["feature"], mesh.shape["tm"])
    shards = exchanged if sizes == (2, 4, 4) else gathered
    return jax.shard_map(
        shards,
        mesh=mesh,
        in_specs=(
            P("tm", "feature"),
            P("tm", "voxel"),
            P(("feature", "tm"), "voxel"),
            P(),
            P(),
            P(),
            P(),
        ),
        out_specs=P(None, None, "voxel"),
        check_vma=False,
    )
```

```python
import math

import jax
import jax.numpy as jnp
from jax import lax
from jax.experimental import pallas as pl
from jax.experimental.pallas import tpu as pltpu
from jax.sharding import PartitionSpec as P

DELAYS = 8
MAXD = 12
LANES = 128
F32 = jnp.float32
BF16 = jnp.bfloat16


def passed_along(value, axis, steps):
    count = lax.axis_size(axis)
    first, last = (max(0, -steps), min(count, count - steps))
    return lax.ppermute(value, axis, [(source, source + steps) for source in range(first, last)])


def contract_rows(left, right):
    return lax.dot_general(
        left, right, (((0,), (0,)), ((), ())), preferred_element_type=jnp.float32
    )


def scaled_by(rotated, eigvals, ridge_grid, total_rows):
    penalty = 2.0 ** ((ridge_grid.astype(jnp.float32) - 8.0) * 0.5)
    scaled = rotated[None] / (
        math.sqrt(total_rows) * (eigvals[None, :, None] + penalty[:, None, None])
    )
    return scaled.astype(jnp.bfloat16)


def gathered(hidden, bold, panel, eigvals, ridge_grid, delays, runs):
    t_rows = hidden.shape[0]
    d_local = hidden.shape[1]
    v_cols = bold.shape[1]
    total_rows = t_rows * lax.axis_size("tm")
    first = lax.axis_index("tm") * t_rows
    ahead = passed_along(bold[:MAXD], "tm", -1)
    extended = jnp.concatenate([bold, ahead], 0)
    runs_pad = jnp.concatenate([runs, jnp.full((MAXD,), -1, jnp.int32)])
    own_runs = lax.dynamic_slice_in_dim(runs, first, t_rows)
    positions = first + jnp.arange(t_rows, dtype=jnp.int32)
    lagged_list = []
    for slot in range(DELAYS):
        offset = delays[slot]
        target_runs = lax.dynamic_slice_in_dim(runs_pad, first + offset, t_rows)
        valid = (positions + offset < total_rows) & (target_runs == own_runs)
        moved = lax.dynamic_slice_in_dim(extended, offset, t_rows, 0)
        lagged_list.append(jnp.where(valid[:, None], moved, jnp.zeros_like(moved)))
    stacked = jnp.stack(lagged_list, 1).reshape(t_rows, DELAYS * v_cols)
    cross = contract_rows(hidden, stacked)
    partial_cov = cross.reshape(d_local * DELAYS, v_cols).astype(jnp.bfloat16)
    panel_rows = lax.all_gather(panel, "tm", axis=0, tiled=True)
    rotated_part = contract_rows(
        lax.all_gather(panel_rows, "voxel", axis=1, tiled=True), partial_cov
    )
    rotated = lax.psum(rotated_part.astype(jnp.bfloat16), ("feature", "tm")).astype(jnp.float32)
    return scaled_by(rotated, eigvals, ridge_grid, total_rows)


def swapped(value, voxel, feature, tm):
    sizes = (lax.axis_size("voxel"), lax.axis_size("feature"), lax.axis_size("tm"))
    pairs = []
    for v in range(sizes[0]):
        for f in range(sizes[1]):
            for t in range(sizes[2]):
                source = (v * sizes[1] + f) * sizes[2] + t
                target = ((v ^ voxel) * sizes[1] + (f ^ feature)) * sizes[2] + (t ^ tm)
                pairs.append((source, target))
    return lax.ppermute(value, ("voxel", "feature", "tm"), pairs)


GROUPS = 4


def as_sent(value):
    return lax.reduce_precision(value, 8, 7)


def received(value, voxel, feature, tm):
    return swapped(value.astype(BF16), voxel, feature, tm).astype(F32)


def sort_matrices(sort):
    width = LANES // GROUPS
    row = lax.broadcasted_iota(jnp.int32, (sort.shape[1], LANES), 0)
    lane = lax.broadcasted_iota(jnp.int32, (sort.shape[1], LANES), 1)
    gap = row - DELAYS * (lane % width)
    for n in range(GROUPS):
        slot = (lane // width - n) % GROUPS
        for t in range(DELAYS // GROUPS):
            sort[n, :, t * LANES:(t + 1) * LANES] = (gap - slot == GROUPS * t).astype(F32).astype(BF16)


def sort_into(ordered, panel_t, sort):
    rows = panel_t.shape[0]
    block = sort.shape[1]
    width = LANES // GROUPS
    tiles = panel_t.shape[1] // (GROUPS * block)
    mixed = [
        jnp.dot(
            jnp.concatenate(
                [panel_t[:, (GROUPS * m + n) * block:(GROUPS * m + n + 1) * block] for m in range(tiles)], 0
            ),
            sort[n], preferred_element_type=F32,
        )
        for n in range(GROUPS)
    ]
    lane = lax.broadcasted_iota(jnp.int32, (rows, LANES), 1)
    for m in range(tiles):
        for t in range(DELAYS // GROUPS):
            parts = [part[m * rows:(m + 1) * rows, t * LANES:(t + 1) * LANES] for part in mixed]
            for r in range(GROUPS):
                tile = parts[(GROUPS - 1 - r) % GROUPS]
                for place in range(GROUPS - 2, -1, -1):
                    tile = jnp.where(lane < (place + 1) * width, parts[(place - r) % GROUPS], tile)
                if r:
                    tile = pltpu.roll(tile, LANES - r * width, 1)
                k = t * GROUPS + r
                ordered[k * rows:(k + 1) * rows, m * LANES:(m + 1) * LANES] = tile.astype(BF16)


def lag_sums(products, valid, shift, total):
    p_cols = total.shape[0]
    tiles = products.shape[1] // LANES
    places = valid.shape[0] // DELAYS
    stacked = []
    for j in range(tiles):
        parts = []
        for k in range(DELAYS):
            mask = valid[k * places + j:k * places + j + 1, :]
            part = products[k * p_cols:(k + 1) * p_cols, j * LANES:(j + 1) * LANES]
            parts.append((part * mask).astype(BF16))
        stacked.append(jnp.concatenate(parts, 1))
    moved = jnp.dot(jnp.concatenate(stacked, 0), shift[...], preferred_element_type=F32)
    for j in range(tiles + 1):
        at = slice(j * LANES, (j + 1) * LANES)
        add = total[:, at]
        if j < tiles:
            add = add + moved[j * p_cols:(j + 1) * p_cols, :LANES]
        if j > 0:
            add = add + moved[(j - 1) * p_cols:j * p_cols, LANES:]
        total[:, at] = add


def product(ordered, hidden):
    return lax.dot_general(
        ordered[...], hidden[...], (((1,), (1,)), ((), ())), preferred_element_type=F32
    )


def feature_copy(hidden, block, target, sem):
    width = target.shape[1]
    return pltpu.make_async_copy(
        hidden.at[:, pl.ds(pl.multiple_of(block * width, width), width)], target, sem
    )


def early_kernel(
    delays_in, panel_t, panel_core, hidden, runs, total, sort, valid, shift,
    delays, here, all_valid, products, ordered, loaded, hidden_own, hidden_core, sems,
):
    rows = hidden.shape[0]
    tiles, kept = rows // LANES, valid.shape[0] // DELAYS
    tm = lax.axis_index("tm")
    copies = [
        pltpu.make_async_copy(delays_in, delays, sems.at[0]),
        pltpu.make_async_copy(runs, here, sems.at[1]),
        pltpu.make_async_copy(panel_t, loaded, sems.at[2]),
        feature_copy(hidden, tm, hidden_own, sems.at[3]),
        feature_copy(hidden, tm ^ 1, hidden_core, sems.at[4]),
    ]
    for copy in copies:
        copy.start()
    sort_matrices(sort)
    total[...] = jnp.zeros_like(total)
    copies[2].wait()
    sort_into(ordered, loaded[...], sort)
    copies[3].wait()
    products[...] = product(ordered, hidden_own)
    sort_into(ordered, panel_core[...], sort)
    copies[0].wait()
    copies[1].wait()
    places = here.shape[0]
    now = here[...]
    place = lax.broadcasted_iota(jnp.int32, now.shape, 0)
    lane = lax.broadcasted_iota(jnp.int32, now.shape, 1)
    later = jnp.where(place == places - 1, -1, pltpu.roll(now, places - 1, 0))
    row = lax.broadcasted_iota(jnp.int32, (LANES, 2 * LANES), 0)
    col = lax.broadcasted_iota(jnp.int32, (LANES, 2 * LANES), 1)
    for k in range(DELAYS):
        back = LANES - delays[k]
        target = jnp.where(lane < back, pltpu.roll(now, back, 1), pltpu.roll(later, back, 1))
        all_valid[k * places:(k + 1) * places, :] = (target == now).astype(F32)
        valid[k * kept:k * kept + tiles, :] = all_valid[pl.ds(k * places + tm * tiles, tiles), :]
        shift[k * LANES:(k + 1) * LANES, :] = (col - row == delays[k]).astype(F32).astype(BF16)
    copies[4].wait()
    products[...] += product(ordered, hidden_core)
    lag_sums(products, valid, shift, total)


def add_part(panel_t, sort, hidden, valid, shift, total, ordered, products):
    sort_into(ordered, panel_t[...], sort)
    products[...] = product(ordered, hidden)
    lag_sums(products, valid, shift, total)


def own_kernel(panel_t, sort, hidden, valid, shift, earlier, total, ordered, products):
    total[...] = earlier[...]
    add_part(panel_t, sort, hidden, valid, shift, total, ordered, products)


def late_kernel(
    panel_t, sort, hidden, valid, shift, earlier, bold, bold_x, ahead, out, ordered, products, total,
):
    rows, v_cols = bold.shape
    total[...] = earlier[...]
    add_part(panel_t, sort, hidden, valid, shift, total, ordered, products)
    mine = total[:, :rows].astype(BF16)
    beyond = total[:, rows:].astype(BF16)
    blank = jnp.zeros((LANES - ahead.shape[0], v_cols), BF16)
    for place, part in enumerate((bold, bold_x)):
        cols = slice(place * v_cols, (place + 1) * v_cols)
        out[:, cols] = jnp.dot(mine, part[...], preferred_element_type=F32) + jnp.dot(
            beyond, jnp.concatenate([ahead[:, cols], blank], 0), preferred_element_type=F32
        )


def head_kernel(bold, bold_x, head):
    v_cols = bold.shape[1]
    for place, part in enumerate((bold, bold_x)):
        head[:, place * v_cols:(place + 1) * v_cols] = part[:16, :]


PARTS = 8


def scale_kernel(rotated, scale, out, scaled, sems):
    step = scaled.shape[0] // PARTS
    total = rotated[...]
    copies = []
    for part in range(PARTS):
        for r in range(part * step, (part + 1) * step):
            scaled[r] = (total * scale[r]).astype(BF16)
        rows = pl.ds(part * step, step)
        copies.append(pltpu.make_async_copy(scaled.at[rows], out.at[rows], sems.at[part]))
        copies[-1].start()
    for copy in copies:
        copy.wait()


def call(kernel, operands, out_shape, scratch, outside=()):
    hbm = pl.BlockSpec(memory_space=pltpu.HBM)
    operands = [
        pltpu.with_memory_space_constraint(operand, pltpu.HBM) if n in outside else operand
        for n, operand in enumerate(operands)
    ]
    vmem = pl.BlockSpec(memory_space=pltpu.VMEM)
    return pl.pallas_call(
        kernel,
        out_shape=out_shape,
        in_specs=[
            hbm if n in outside else vmem
            for n, operand in enumerate(operands)
        ],
        out_specs=jax.tree.map(lambda _: vmem, out_shape),
        scratch_shapes=scratch,
        compiler_params=pltpu.CompilerParams(vmem_limit_bytes=12 * 1024 * 1024),
        cost_estimate=pl.CostEstimate(flops=1024, bytes_accessed=1024, transcendentals=0),
    )(*operands)


def after(value, done):
    return lax.optimization_barrier((value, done))[0]


def exchanged(hidden, bold, panel, eigvals, ridge_grid, delays, runs):
    t_rows, d_local = hidden.shape
    v_cols = bold.shape[1]
    p_cols = panel.shape[1]
    tm_count = lax.axis_size("tm")
    total_rows = t_rows * tm_count
    width = d_local // tm_count
    block = DELAYS * LANES
    tm = lax.axis_index("tm")
    voxel = lax.axis_index("voxel")
    reach = t_rows + LANES
    dma = pltpu.SemaphoreType.DMA

    panel_t = panel.T
    late_t = swapped(panel_t, 0, 0, 3)
    panel_core = swapped(panel_t, 0, 0, 1)
    bold_x = swapped(bold, 1, 0, 0)

    places = runs.shape[0] // LANES
    features = pltpu.VMEM((t_rows, width), BF16)
    ordered = pltpu.VMEM((DELAYS * p_cols, width), BF16)
    products = pltpu.VMEM((DELAYS * p_cols, t_rows), F32)
    total = jax.ShapeDtypeStruct((p_cols, reach), F32)
    earlier, sort, valid, shift = call(
        early_kernel, (delays, panel_t, panel_core, hidden, runs.reshape(places, LANES)),
        (total, jax.ShapeDtypeStruct((GROUPS, block // GROUPS, block // GROUPS), BF16),
         jax.ShapeDtypeStruct((DELAYS * -(-t_rows // (8 * LANES)) * 8, LANES), F32), jax.ShapeDtypeStruct((block, 2 * LANES), BF16)),
        [pltpu.SMEM(delays.shape, jnp.int32), pltpu.VMEM((places, LANES), jnp.int32),
         pltpu.VMEM((DELAYS * places, LANES), F32),
         products, ordered, pltpu.VMEM(panel_t.shape, BF16), features, features, dma((5,))], (0, 1, 3, 4),
    )
    penalty = 2.0 ** ((ridge_grid.astype(F32) - 8.0) * 0.5)
    scale = 1.0 / (math.sqrt(total_rows) * (eigvals[None, :] + penalty[:, None]))
    scale = jnp.broadcast_to(scale[:, :, None], (*scale.shape, v_cols))
    head = call(
        head_kernel, (bold, after(bold_x, earlier)), jax.ShapeDtypeStruct((16, 2 * v_cols), BF16), []
    )
    ahead = passed_along(head, "tm", -1)
    hidden_late = after(hidden, (head, scale))
    hidden_own = lax.dynamic_slice_in_dim(hidden_late, (tm ^ 3) * width, width, 1)
    hidden_core = lax.dynamic_slice_in_dim(hidden_late, (tm ^ 2) * width, width, 1)
    late_t = after(late_t, (ahead, hidden_own, hidden_core))
    late_core = swapped(late_t, 0, 0, 1)
    earlier = call(
        own_kernel, (late_t, sort, hidden_own, valid, shift, earlier), total, [ordered, products]
    )
    part = call(
        late_kernel,
        (after(late_core, earlier), sort, hidden_core, valid, shift, earlier, bold, bold_x, ahead),
        jax.ShapeDtypeStruct((p_cols, 2 * v_cols), F32),
        [ordered, products, pltpu.VMEM((p_cols, reach), F32)],
    )

    part = as_sent(part)
    part = as_sent(part + received(part, 0, 0, 1)).astype(BF16)
    mine, theirs = part[:, :v_cols], part[:, v_cols:]
    from_x = swapped(theirs.astype(BF16), 1, 0, 1)
    from_xy = swapped(theirs.astype(BF16), 1, 0, 3)
    from_y = swapped(mine.astype(BF16), 0, 0, 3)
    from_y, from_x, from_xy = lax.optimization_barrier((from_y, from_x, from_xy))
    near = mine.astype(F32) + from_y.astype(F32)
    far = from_x.astype(F32) + from_xy.astype(F32)
    rotated = jnp.where(
        voxel == 0, jnp.concatenate([near, far], 0), jnp.concatenate([far, near], 0)
    )
    for step in (1, 2):
        rotated = as_sent(rotated)
        rotated = rotated + received(rotated, 0, step, 1)
    shape = (ridge_grid.shape[0], 2 * p_cols, v_cols)
    return pl.pallas_call(
        scale_kernel,
        out_shape=jax.ShapeDtypeStruct(shape, BF16),
        in_specs=2 * [pl.BlockSpec(memory_space=pltpu.VMEM)],
        out_specs=pl.BlockSpec(memory_space=pl.ANY),
        scratch_shapes=[pltpu.VMEM(shape, BF16), dma((PARTS,))],
        compiler_params=pltpu.CompilerParams(vmem_limit_bytes=4 * 1024 * 1024),
    )(rotated, scale)


def solution(mesh):
    sizes = (mesh.shape["voxel"], mesh.shape["feature"], mesh.shape["tm"])
    shards = exchanged if sizes == (2, 4, 4) else gathered
    return jax.shard_map(
        shards,
        mesh=mesh,
        in_specs=(
            P("tm", "feature"),
            P("tm", "voxel"),
            P(("feature", "tm"), "voxel"),
            P(),
            P(),
            P(),
            P(),
        ),
        out_specs=P(None, None, "voxel"),
        check_vma=False,
    )
```
